128 devices in a mesh: expert: 16 (over y, z), tensor: 8 (over x, core).
Axes of the slice: x: 4, y: 4, z: 4, core: 2. Of those that a mesh axis runs over, the one named last changes fastest.
Arguments:
- tokens: bfloat16 [2048, 4096], P('expert'), may hold values from -6 to 6
- cotangent: bfloat16 [2048, 4096], P('expert'), may hold values from -1.5 to 1.5
- gate_values: bfloat16 [2048, 8], P('expert'), may hold values from 0.19921875 to 1
- expert_ids: int32 [2048, 8], P('expert'), may hold values from 0 to 31, all different within a row; in each aligned block of 128 rows (0 to 127, 128 to 255, ...) at most 36 rows name the same one
- w_gate: bfloat16 [32, 1536, 4096], P('expert', 'tensor'), may hold values from -0.09375 to 0.09375
- w_up: bfloat16 [32, 1536, 4096], P('expert', 'tensor'), may hold values from -0.09375 to 0.09375
- w_down: bfloat16 [32, 1536, 4096], P('expert', 'tensor'), may hold values from -0.15625 to 0.15625
Outputs:
- d_tokens: bfloat16 [2048, 4096], P('expert', 'tensor')
- d_gates: bfloat16 [2048, 8], P('expert')
- d_w_gate: bfloat16 [32, 1536, 4096], P('expert', 'tensor')
- d_w_up: bfloat16 [32, 1536, 4096], P('expert', 'tensor')
- d_w_down: bfloat16 [32, 1536, 4096], P('expert', 'tensor')
The draws below stay inside these ranges and needn't reach their ends.
Inputs may be any that keep to these rules, and one draw needn't show every extreme that they name: `expert_ids`: each row names 8 different experts. In each aligned block of 128 rows no expert is named by more than 36 rows, a bound that some block reaches.
All inputs are finite; a program needn't handle non-finite values.
Results may differ from the reference program's by a relative error of at most 0.02.
Values may be sent and summed in bfloat16 or wider, within the bound.
No kernel may reach another device: no remote copies, remote signals or barrier semaphores. Data moves between devices by JAX's collectives and lax.ppermute only.
A program may use at most 192 MiB of HBM per device.

```python
import math
import jax
import jax.numpy as jnp
import numpy as np
from jax import lax

D = 4096
FF = 1536
TOPK = 8
TOK_GRP = 128
EXPERTS = 32
TOKENS = 2048
CAP = 36
N_EXPERT = 16
N_TENSOR = 8


def block_scale(stream_key, extent, pieces, least, largest):
    def one(axis_at, blocks):
        steps = jax.random.uniform(jax.random.fold_in(jax.random.fold_in(stream_key, 6), axis_at), (blocks,), jnp.float32, least / len(pieces), largest / len(pieces))
        return jnp.repeat(jnp.exp(steps), extent[axis_at] // blocks).reshape((-1,) + (1,) * (len(extent) - axis_at - 1))

    gain = one(*pieces[0])
    for cut in pieces[1:]:
        gain = gain * one(*cut)
    return gain


def deal_out(key, own, number, rows, count, top, reach, slope):
    sequence = jax.random.permutation(key, count)
    crowded, common = shares(count, rows * top, reach, slope, True), shares(count, rows * top, reach, slope, False)
    places = jnp.arange(count)

    def named(tallies, offset_by):
        used = int((tallies > 0).sum())
        fixed = max(1, used // 4)
        moved = fixed + (places - fixed + offset_by * (used - fixed)) % max(1, count - fixed)
        return jnp.zeros((count,), jnp.int32).at[sequence[jnp.where(places < fixed, places, moved)]].set(jnp.asarray(tallies, jnp.int32))

    tallies = jnp.where(number % 4 == 0, named(crowded, number // 4), named(common, number - number // 4 - 1))
    mixed = jax.random.permutation(jax.random.fold_in(own, 3), count)
    giver, receiver = mixed[0:count // 2 * 2:2], mixed[1:count // 2 * 2:2]
    room = jnp.minimum(tallies[giver] - 1, reach - tallies[receiver]) // 2
    room = jnp.where((giver == sequence[0]) | (receiver == sequence[0]) | (tallies[receiver] == 0), 0, jnp.maximum(room, 0))
    moved = jax.random.randint(jax.random.fold_in(own, 4), (count // 2,), 0, 1 << 20) % (room + 1)
    tallies = tallies.at[giver].add(-moved).at[receiver].add(moved)
    items = jnp.searchsorted(jnp.cumsum(tallies), jnp.arange(rows * top), side="right").astype(jnp.int32)
    listing = items.reshape(top, rows).T
    listing = listing[jax.random.permutation(jax.random.fold_in(own, 1), rows)]
    offset_by = jax.random.randint(jax.random.fold_in(own, 2), (rows, 1), 0, top)
    return jnp.take_along_axis(listing, (jnp.arange(top)[None, :] + offset_by) % top, axis=1)


def shares(amount, total, reach, lean, full):
    loads = [(1 << 20) // math.isqrt(grade ** lean) + 1 for grade in range(1, amount + 1)]
    largest = reach if full else min(reach, max(-(-total // amount), total * loads[0] // sum(loads)))
    least = 1 if total - largest >= amount - 1 else 0
    given, rest = [largest] + [least] * (amount - 1), total - largest - least * (amount - 1)
    while rest > 0:
        free = [i for i in range(1, amount) if given[i] < largest] or [i for i in range(1, amount) if given[i] < reach]
        mass, remaining = sum([loads[i] for i in free]), rest
        for i in free:
            extra = min(reach - given[i], max(1, remaining * loads[i] // mass), rest)
            given[i] = given[i] + extra
            rest = rest - extra
    return np.array(given)


def bell_draw(key, shape, spread, reach, shards=(), kind=jnp.bfloat16):
    result = spread * jax.random.normal(key, shape, jnp.float32)
    if shards:
        result = result * block_scale(key, shape, shards, -0.22, 0.18)
    return jnp.clip(result, -reach, reach).astype(kind)


def setup_inputs(seed: int = 0) -> dict:
    key_of = jax.random.split(jax.random.key(seed), 8)
    tokens = bell_draw(key_of[0], (TOKENS, D), 1.0, 6.0, ((0, 16),))
    cotangent = bell_draw(key_of[1], (TOKENS, D), 0.25, 1.5, ((0, 16),))
    gate_values = jnp.clip(0.19921875 + 0.80078125 * jax.random.uniform(key_of[2], (TOKENS, TOPK), jnp.float32) ** block_scale(key_of[2], (TOKENS, TOPK), ((0, 16),), -0.2, 0.2), 0.19921875, 1.0).astype(jnp.bfloat16)
    expert_ids_keys = jax.random.split(jax.random.fold_in(key_of[3], 1), TOKENS // TOK_GRP)
    expert_ids_turns = jax.random.permutation(jax.random.fold_in(key_of[3], 3), TOKENS // TOK_GRP)
    expert_ids = jax.vmap(lambda own, number: deal_out(jax.random.fold_in(key_of[3], 2), own, number, TOK_GRP, EXPERTS, TOPK, CAP, 1))(expert_ids_keys, expert_ids_turns).reshape((TOKENS, TOPK))
    w_gate = bell_draw(key_of[4], (EXPERTS, FF, D), D ** -0.5, 0.09375, ((0, 16), (1, 8)))
    w_up = bell_draw(key_of[5], (EXPERTS, FF, D), D ** -0.5, 0.09375, ((0, 16), (1, 8)))
    w_down = bell_draw(key_of[6], (EXPERTS, FF, D), FF ** -0.5, 0.15625, ((0, 16), (1, 8)))
    return {"tokens": tokens, "cotangent": cotangent, "gate_values": gate_values, "expert_ids": expert_ids, "w_gate": w_gate, "w_up": w_up, "w_down": w_down}


def slot_table(group_ids):
    flat_ids = group_ids.reshape(-1)
    entries = flat_ids.shape[0]
    one_hot = (flat_ids[:, None] == jnp.arange(EXPERTS, dtype=jnp.int32)[None, :]).astype(jnp.int32)
    running = jnp.cumsum(one_hot, axis=0)
    position = jnp.sum((running - 1) * one_hot, axis=1).astype(jnp.int32)
    slot_index = flat_ids * CAP + position
    entry_table = jnp.full((EXPERTS * CAP,), entries, jnp.int32).at[slot_index].set(jnp.arange(entries, dtype=jnp.int32))
    return entry_table.reshape(EXPERTS, CAP), position.reshape(group_ids.shape)


def expert_pass(operands):
    x_rows, dy_rows, g_rows, gate_w, up_w, down_w = operands
    gate_pre = jnp.dot(x_rows, gate_w.T, preferred_element_type=jnp.float32)
    up_pre = jnp.dot(x_rows, up_w.T, preferred_element_type=jnp.float32)
    sigma_gate = jax.nn.sigmoid(gate_pre)
    hidden = (gate_pre * sigma_gate * up_pre).astype(jnp.bfloat16)
    expert_out = jnp.dot(hidden, down_w, preferred_element_type=jnp.float32)
    slot_score = jnp.sum(dy_rows.astype(jnp.float32) * expert_out, axis=1)
    scaled = (g_rows.astype(jnp.float32)[:, None] * dy_rows.astype(jnp.float32)).astype(jnp.bfloat16)
    d_hidden = jnp.dot(scaled, down_w.T, preferred_element_type=jnp.float32)
    d_gate_pre = (d_hidden * up_pre * sigma_gate * (1.0 + gate_pre * (1.0 - sigma_gate))).astype(jnp.bfloat16)
    d_up_pre = (d_hidden * gate_pre * sigma_gate).astype(jnp.bfloat16)
    grad_gate = jnp.dot(d_gate_pre.T, x_rows, preferred_element_type=jnp.float32).astype(jnp.bfloat16)
    grad_up = jnp.dot(d_up_pre.T, x_rows, preferred_element_type=jnp.float32).astype(jnp.bfloat16)
    grad_down = jnp.dot(hidden.T, scaled, preferred_element_type=jnp.float32).astype(jnp.bfloat16)
    block_width = FF // N_TENSOR
    total = jnp.zeros((x_rows.shape[0], D), jnp.float32)
    for block in range(N_TENSOR):
        low = block * block_width
        high = low + block_width
        partial_sum = jnp.dot(d_gate_pre[:, low:high], gate_w[low:high, :], preferred_element_type=jnp.float32)
        partial_sum = partial_sum + jnp.dot(d_up_pre[:, low:high], up_w[low:high, :], preferred_element_type=jnp.float32)
        total = total + lax.optimization_barrier(partial_sum.astype(jnp.bfloat16)).astype(jnp.float32)
    return grad_gate, grad_up, grad_down, total.astype(jnp.bfloat16), slot_score


def reference(tokens, cotangent, gate_values, expert_ids, w_gate, w_up, w_down):
    entries = TOK_GRP * TOPK
    groups = expert_ids.reshape(N_EXPERT, TOK_GRP, TOPK)
    entry_table, position = jax.vmap(slot_table)(groups)
    is_live = entry_table < entries
    safe_entry = jnp.minimum(entry_table, entries - 1)
    group_index = jnp.arange(N_EXPERT, dtype=jnp.int32)[:, None, None]
    global_row = group_index * TOK_GRP + safe_entry // TOPK
    zero = jnp.zeros((), tokens.dtype)
    x_slot = jnp.where(is_live[..., None], tokens[global_row], zero)
    dy_slot = jnp.where(is_live[..., None], cotangent[global_row], zero)
    g_slot = jnp.where(is_live, gate_values.reshape(-1)[group_index * entries + safe_entry], zero)
    x_exp = jnp.moveaxis(x_slot, 1, 0).reshape(EXPERTS, N_EXPERT * CAP, D)
    dy_exp = jnp.moveaxis(dy_slot, 1, 0).reshape(EXPERTS, N_EXPERT * CAP, D)
    g_exp = jnp.moveaxis(g_slot, 1, 0).reshape(EXPERTS, N_EXPERT * CAP)
    grad_gate, grad_up, grad_down, dx_slot, slot_score = lax.map(expert_pass, (x_exp, dy_exp, g_exp, w_gate, w_up, w_down))
    dx_slot = dx_slot.reshape(EXPERTS, N_EXPERT, CAP, D)
    slot_score = slot_score.reshape(EXPERTS, N_EXPERT, CAP)
    picked = dx_slot[groups, group_index, position]
    d_tokens = jnp.sum(picked.astype(jnp.float32), axis=2).astype(jnp.bfloat16).reshape(TOKENS, D)
    d_gates = slot_score[groups, group_index, position].astype(jnp.bfloat16).reshape(TOKENS, TOPK)
    return d_tokens, d_gates, grad_gate, grad_up, grad_down
```

```python
import functools

import jax
import jax.numpy as jnp
from jax import lax
from jax.experimental import pallas as pl
from jax.experimental.pallas import tpu as pltpu
from jax.sharding import PartitionSpec as P

BF = jnp.bfloat16
F32 = jnp.float32
SIDE = 4
OFFS = (0, 3, 1, 2)
CAP = 36
ROWS = SIDE * SIDE * CAP
BAND = SIDE * CAP
VMEM = 56 * 1024 * 1024


def dot(a, b):
    return lax.dot_general(a, b, (((1,), (0,)), ((), ())), preferred_element_type=F32)


def dot_t(a, b):
    return lax.dot_general(a, b, (((1,), (1,)), ((), ())), preferred_element_type=F32)


def shift(v, axis, step):
    perm = []
    for y in range(SIDE):
        for z in range(SIDE):
            to = ((y + step) % SIDE, z) if axis == "y" else (y, (z + step) % SIDE)
            perm.append((y * SIDE + z, to[0] * SIDE + to[1]))
    return lax.ppermute(v, "expert", perm)


def swap_core(v):
    n = lax.axis_size("tensor")
    return lax.ppermute(v, "tensor", [(i, i ^ 1) for i in range(n)])


def ring(v, axis):
    half = v.shape[0] // 2
    before = shift(v, axis, 1)
    after = shift(v, axis, -1)
    far_low = shift(before[:half], axis, 1)
    far_high = shift(after[half:], axis, -1)
    return (v, before, after, far_low, far_high)


def gather_groups(a, b):
    a1 = jnp.concatenate(ring(a, "z"), 0)
    b1 = jnp.concatenate(ring(b, "y"), 0)
    return ring(a1, "y"), ring(b1, "z")


def pack_kernel(tg, pos_ref, a0, a1, a2, a3, a4, b0, b1, b2, b3, b4, pick_ref, out_ref):
    y = pos_ref[0]
    width = a0.shape[1]
    a_parts = (a0, a1, a2, (a3, a4))
    half = SIDE // 2
    for j, off in enumerate(OFFS):
        row = lax.rem(y + off, SIDE)
        if j < 3:
            a = a_parts[j][...]
        else:
            a = jnp.concatenate([a3[...], a4[...]], 0)
        far, at = (b3, j) if j < half else (b4, j - half)
        b = jnp.concatenate(
            [r[j * tg : (j + 1) * tg, :] for r in (b0, b1, b2)] + [far[at * tg : (at + 1) * tg, :]],
            0,
        )
        start = pl.multiple_of(row * BAND, 16)
        for e in range(2):
            pick = pick_ref[e, row]
            out_ref[e, pl.ds(start, BAND), :width] = dot(pick, a).astype(BF)
            out_ref[e, pl.ds(start, BAND), width:] = dot(pick, b).astype(BF)


def pack_rows(pos, a_parts, b_parts, pick, blk, feats):
    tg = a_parts[0].shape[0] // SIDE
    specs = [pl.BlockSpec((p.shape[0], blk), lambda f, s: (0, f)) for p in a_parts + b_parts]
    return pl.pallas_call(
        functools.partial(pack_kernel, tg),
        out_shape=jax.ShapeDtypeStruct((2, ROWS, feats), BF),
        grid_spec=pltpu.PrefetchScalarGridSpec(
            num_scalar_prefetch=1,
            grid=(feats // (2 * blk),),
            in_specs=specs + [pl.BlockSpec(pick.shape, lambda f, s: (0, 0, 0, 0))],
            out_specs=pl.BlockSpec((2, ROWS, 2 * blk), lambda f, s: (0, 0, f)),
        ),
        compiler_params=pltpu.CompilerParams(vmem_limit_bytes=VMEM),
        cost_estimate=pl.CostEstimate(
            flops=2 * 2 * ROWS * SIDE * tg * feats, transcendentals=0, bytes_accessed=14 * 2**20
        ),
        name="pack",
    )(pos, *a_parts, *b_parts, pick)


def own_at(n):
    return lambda e, j, s: (e, 0, jnp.minimum(j, n - 1))


def other_at(n):
    return lambda e, j, s: (e, 0, jnp.maximum(j - n, 0))


def col_at(n):
    def at(e, j, s):
        first = j < n
        core = jnp.where(first, s[1], 1 - s[1])
        return (e, 0, core * n + jnp.where(first, j, j - n))

    return at


def pre_kernel(n, pos_ref, own, other, wg, wu, gate_ref, up_ref):
    j = pl.program_id(1)

    @pl.when(j == 0)
    def _():
        gate_ref[...] = jnp.zeros_like(gate_ref)
        up_ref[...] = jnp.zeros_like(up_ref)

    def add(x):
        gate_ref[0] += dot_t(x, wg[0])
        up_ref[0] += dot_t(x, wu[0])

    @pl.when(j < n)
    def _():
        add(own[0])

    @pl.when(j >= n)
    def _():
        add(other[0])


def pre_rows(pos, own, other, w_gate, w_up, blk=1024):
    hid = w_gate.shape[1]
    n = own.shape[2] // blk
    return pl.pallas_call(
        functools.partial(pre_kernel, n),
        out_shape=[jax.ShapeDtypeStruct((2, ROWS, hid), F32)] * 2,
        grid_spec=pltpu.PrefetchScalarGridSpec(
            num_scalar_prefetch=1,
            grid=(2, 2 * n),
            in_specs=[
                pl.BlockSpec((1, ROWS, blk), own_at(n)),
                pl.BlockSpec((1, ROWS, blk), other_at(n)),
                pl.BlockSpec((1, hid, blk), col_at(n)),
                pl.BlockSpec((1, hid, blk), col_at(n)),
            ],
            out_specs=[pl.BlockSpec((1, ROWS, hid), lambda e, j, s: (e, 0, 0))] * 2,
        ),
        compiler_params=pltpu.CompilerParams(vmem_limit_bytes=VMEM),
        cost_estimate=pl.CostEstimate(
            flops=2 * 4 * ROWS * hid * n * 2 * blk, transcendentals=0, bytes_accessed=18 * 2**20
        ),
        name="pre",
    )(pos, own, other, w_gate, w_up)


def mid_kernel(n, pos_ref, own, other, wd, gate_ref, up_ref, g_ref, both_ref, both_t, hid_t, score, acc):
    j = pl.program_id(1)

    @pl.when(j == 0)
    def _():
        acc[...] = jnp.zeros_like(acc)

    @pl.when(j < n)
    def _():
        acc[...] += dot_t(own[0], wd[0])

    @pl.when(j >= n)
    def _():
        acc[...] += dot_t(other[0], wd[0])

    @pl.when(j == 2 * n - 1)
    def _():
        gate, up, g = gate_ref[0], up_ref[0], g_ref[0]
        dy = acc[...]
        s = jax.nn.sigmoid(gate)
        act = gate * s
        hidden = act * up
        score[0] = jnp.sum(hidden * dy, axis=1, keepdims=True)
        d_hid = dy * g
        d_up = d_hid * act
        d_gate = d_hid * up * s * (1.0 + gate * (1.0 - s))
        both = jnp.concatenate([d_gate, d_up], 1)
        both_ref[0] = both.astype(BF)
        both_t[0] = both.T.astype(BF)
        hid_t[0] = (hidden * g).T.astype(BF)


def mid_rows(pos, own, other, w_down, gate, up, g, blk=1024):
    hid = w_down.shape[1]
    n = own.shape[2] // blk
    whole = lambda e, j, s: (e, 0, 0)
    return pl.pallas_call(
        functools.partial(mid_kernel, n),
        out_shape=[
            jax.ShapeDtypeStruct((2, ROWS, 2 * hid), BF),
            jax.ShapeDtypeStruct((2, 2 * hid, ROWS), BF),
            jax.ShapeDtypeStruct((2, hid, ROWS), BF),
            jax.ShapeDtypeStruct((2, ROWS, 1), F32),
        ],
        grid_spec=pltpu.PrefetchScalarGridSpec(
            num_scalar_prefetch=1,
            grid=(2, 2 * n),
            in_specs=[
                pl.BlockSpec((1, ROWS, blk), own_at(n)),
                pl.BlockSpec((1, ROWS, blk), other_at(n)),
                pl.BlockSpec((1, hid, blk), col_at(n)),
                pl.BlockSpec((1, ROWS, hid), whole),
                pl.BlockSpec((1, ROWS, hid), whole),
                pl.BlockSpec((1, ROWS, 1), whole),
            ],
            out_specs=[
                pl.BlockSpec((1, ROWS, 2 * hid), whole),
                pl.BlockSpec((1, 2 * hid, ROWS), whole),
                pl.BlockSpec((1, hid, ROWS), whole),
                pl.BlockSpec((1, ROWS, 1), whole),
            ],
            scratch_shapes=[pltpu.VMEM((ROWS, hid), F32)],
        ),
        compiler_params=pltpu.CompilerParams(vmem_limit_bytes=VMEM),
        cost_estimate=pl.CostEstimate(
            flops=2 * 2 * ROWS * hid * n * 2 * blk,
            transcendentals=2 * ROWS * hid,
            bytes_accessed=20 * 2**20,
        ),
        name="mid",
    )(pos, own, other, w_down, gate, up, g)


def dx_kernel(both, wg, wu, out_ref):
    hid = wg.shape[1]
    for e in range(2):
        w = jnp.concatenate([wg[e], wu[e]], 0)
        out_ref[e * ROWS : (e + 1) * ROWS, :] = dot(both[e], w).astype(BF)


def dx_rows(both, w_gate, w_up, blk=512):
    hid, width = w_gate.shape[1:]
    return pl.pallas_call(
        dx_kernel,
        out_shape=jax.ShapeDtypeStruct((2 * ROWS, width), BF),
        grid=(width // blk,),
        in_specs=[
            pl.BlockSpec(both.shape, lambda j: (0, 0, 0)),
            pl.BlockSpec((2, hid, blk), lambda j: (0, 0, j)),
            pl.BlockSpec((2, hid, blk), lambda j: (0, 0, j)),
        ],
        out_specs=pl.BlockSpec((2 * ROWS, blk), lambda j: (0, j)),
        compiler_params=pltpu.CompilerParams(vmem_limit_bytes=VMEM),
        cost_estimate=pl.CostEstimate(
            flops=2 * 4 * ROWS * hid * width, transcendentals=0, bytes_accessed=18 * 2**20
        ),
        name="dx",
    )(both, w_gate, w_up)


def grad_kernel(n, pos_ref, x_own, x_other, y_own, y_other, both_t, hid_t, gg, gu, gd):
    j = pl.program_id(1)
    hid = gg.shape[1]

    def put(x, y):
        r = dot(both_t[0], x)
        gg[0] = r[:hid].astype(BF)
        gu[0] = r[hid:].astype(BF)
        gd[0] = dot(hid_t[0], y).astype(BF)

    @pl.when(j < n)
    def _():
        put(x_own[0], y_own[0])

    @pl.when(j >= n)
    def _():
        put(x_other[0], y_other[0])


def grad_rows(pos, x_own, x_other, y_own, y_other, both_t, hid_t, blk=1024):
    hid = hid_t.shape[1]
    n = x_own.shape[2] // blk
    whole = lambda e, j, s: (e, 0, 0)
    return pl.pallas_call(
        functools.partial(grad_kernel, n),
        out_shape=[jax.ShapeDtypeStruct((2, hid, 2 * n * blk), BF)] * 3,
        grid_spec=pltpu.PrefetchScalarGridSpec(
            num_scalar_prefetch=1,
            grid=(2, 2 * n),
            in_specs=[
                pl.BlockSpec((1, ROWS, blk), own_at(n)),
                pl.BlockSpec((1, ROWS, blk), other_at(n)),
                pl.BlockSpec((1, ROWS, blk), own_at(n)),
                pl.BlockSpec((1, ROWS, blk), other_at(n)),
                pl.BlockSpec((1, 2 * hid, ROWS), whole),
                pl.BlockSpec((1, hid, ROWS), whole),
            ],
            out_specs=[pl.BlockSpec((1, hid, blk), col_at(n))] * 3,
        ),
        compiler_params=pltpu.CompilerParams(vmem_limit_bytes=VMEM),
        cost_estimate=pl.CostEstimate(
            flops=2 * 6 * ROWS * hid * n * 2 * blk, transcendentals=0, bytes_accessed=30 * 2**20
        ),
        name="grads",
    )(pos, x_own, x_other, y_own, y_other, both_t, hid_t)


def before_count(member):
    t = member.shape[-1]
    upper = (jnp.arange(t)[:, None] < jnp.arange(t)[None, :]).astype(BF)
    return jnp.dot(member.astype(BF), upper, preferred_element_type=F32).astype(jnp.int32)


def on_device(tokens, cotangent, gate_values, expert_ids, w_gate, w_up, w_down):
    tg, top = expert_ids.shape
    width = tokens.shape[1]
    n_exp = lax.axis_size("expert")
    experts = 2 * n_exp
    me = lax.axis_index("expert")
    lane = lax.axis_index("tensor")
    y, z, core = me // SIDE, me % SIDE, lane % 2
    pos = jnp.stack([y, core]).astype(jnp.int32)
    feats = width // 2
    blk = 256

    def cut(v):
        mine = lax.dynamic_slice_in_dim(v, core * feats, feats, 1)
        mine = mine.reshape(tg, feats // (2 * blk), 2, blk)
        return mine[:, :, 0].reshape(tg, feats // 2), mine[:, :, 1].reshape(tg, feats // 2)

    xa, xb = cut(tokens)
    ya, yb = cut(cotangent)
    route = jnp.concatenate([expert_ids.astype(BF), gate_values], 1)
    route = jnp.pad(route, ((0, 0), (0, 128 - 2 * top)))
    xa = jnp.concatenate([xa, route], 1)
    xa_parts, xb_parts = gather_groups(xa, xb)
    ya_parts, yb_parts = gather_groups(ya, yb)

    tab = jnp.concatenate([p[:, feats // 2 : feats // 2 + 2 * top] for p in xa_parts], 0)
    tab = tab.reshape(SIDE, SIDE, tg, 2 * top)
    offs = jnp.array(OFFS, jnp.int32)
    tab = tab[jnp.array((0, 2, 3, 1))[(jnp.arange(SIDE) - y) % SIDE]]
    ids = tab[..., :top].astype(jnp.int32)
    gates = tab[..., top:].astype(F32)
    mine = 2 * me + jnp.arange(2)
    named = ids[None] == mine[:, None, None, None, None]
    member = jnp.any(named, -1)
    weight = jnp.sum(jnp.where(named, gates[None], 0.0), -1)
    count = before_count(member)
    z_abs = (z + offs) % SIDE
    target = jnp.where(member, z_abs[None, None, :, None] * CAP + count, -1)
    target = target.reshape(2, SIDE, 1, SIDE * tg)
    hit = target == jnp.arange(BAND)[None, None, :, None]
    pick = hit.astype(BF)
    g_slot = jnp.sum(jnp.where(hit, weight.reshape(2, SIDE, 1, SIDE * tg), 0.0), -1)
    g_slot = g_slot.reshape(2, ROWS, 1)

    x_own = pack_rows(pos, xa_parts, xb_parts, pick, blk, feats)
    x_other = swap_core(x_own)
    gate_pre, up_pre = pre_rows(pos, x_own, x_other, w_gate, w_up)
    y_own = pack_rows(pos, ya_parts, yb_parts, pick, blk, feats)
    y_other = swap_core(y_own)
    both, both_t, hid_t, score = mid_rows(pos, y_own, y_other, w_down, gate_pre, up_pre, g_slot)
    dx = dx_rows(both, w_gate, w_up)
    share = lax.psum_scatter(dx, "tensor", scatter_dimension=1, tiled=True)
    n_ten = lax.axis_size("tensor")
    total = score.reshape(ROWS * 2 // 128, 128)
    for bit in (1, 2, 4):
        total = total + lax.ppermute(total, "tensor", [(i, i ^ bit) for i in range(n_ten)])
    grad_gate, grad_up, grad_down = grad_rows(pos, x_own, x_other, y_own, y_other, both_t, hid_t)

    part = width // n_ten
    back = share.reshape(2, n_exp, CAP, part).transpose(1, 0, 2, 3).reshape(n_exp, 2 * CAP, part)
    line = total.reshape(2, n_exp, CAP).transpose(1, 0, 2).reshape(n_exp, 1, 2 * CAP).astype(BF)
    line = jnp.pad(line, ((0, 0), (0, 7), (0, part - 2 * CAP)))
    back = jnp.concatenate([back, line], 1)
    back = lax.all_to_all(back, "expert", split_axis=0, concat_axis=0, tiled=True)

    own_named = expert_ids[:, :, None] == jnp.arange(experts)[None, None, :]
    own_member = jnp.any(own_named, 1)
    own_count = before_count(own_member.T).T
    own_hit = own_member[:, :, None] & (own_count[:, :, None] == jnp.arange(CAP)[None, None, :])
    spread = own_hit.astype(BF).reshape(tg, n_exp, 2 * CAP)
    d_tokens = jnp.einsum(
        "tns,nsf->tf", spread, back[:, : 2 * CAP], preferred_element_type=F32
    ).astype(BF)
    scores = back[:, 2 * CAP, : 2 * CAP].reshape(experts, CAP)
    by_expert = jnp.sum(jnp.where(own_hit, scores[None].astype(F32), 0.0), 2)
    d_gates = jnp.sum(jnp.where(own_named, by_expert[:, None, :], 0.0), 2).astype(BF)
    return d_tokens, d_gates, grad_gate, grad_up, grad_down


def solution(mesh):
    placed = (
        P("expert", None),
        P("expert", None),
        P("expert", None),
        P("expert", None),
        P("expert", "tensor", None),
        P("expert", "tensor", None),
        P("expert", "tensor", None),
    )
    return jax.shard_map(
        on_device,
        mesh=mesh,
        in_specs=placed,
        out_specs=(
            P("expert", "tensor"),
            P("expert", None),
            P("expert", "tensor", None),
            P("expert", "tensor", None),
            P("expert", "tensor", None),
        ),
        check_vma=False,
    )
```

```python
import functools

import jax
import jax.numpy as jnp
from jax import lax
from jax.experimental import pallas as pl
from jax.experimental.pallas import tpu as pltpu
from jax.sharding import PartitionSpec as P

BF = jnp.bfloat16
F32 = jnp.float32
SIDE = 4
OFFS = (0, 3, 1, 2)
CAP = 36
ROWS = SIDE * SIDE * CAP
BAND = SIDE * CAP
PAD = 40
MIB = 1024 * 1024


def dot(a, b):
    return lax.dot_general(a, b, (((1,), (0,)), ((), ())), preferred_element_type=F32)


def dot_t(a, b):
    return lax.dot_general(a, b, (((1,), (1,)), ((), ())), preferred_element_type=F32)


def shift(v, axis, step):
    perm = []
    for y in range(SIDE):
        for z in range(SIDE):
            to = ((y + step) % SIDE, z) if axis == "y" else (y, (z + step) % SIDE)
            perm.append((y * SIDE + z, to[0] * SIDE + to[1]))
    return lax.ppermute(v, "expert", perm)


def swap_core(v):
    n = lax.axis_size("tensor")
    return lax.ppermute(v, "tensor", [(i, i ^ 1) for i in range(n)])


def near(v, axis):
    return (v, shift(v, axis, 1), shift(v, axis, -1))


def far(blocks, axis, half=None):
    v, before, after = blocks
    half = half or v.shape[0] // 2
    return (shift(before[:half], axis, 1), shift(after[half:], axis, -1))


def ring(v, axis, half=None):
    blocks = near(v, axis)
    return blocks + far(blocks, axis, half)


def after_all(values, others):
    return lax.optimization_barrier((values, others))[0]


def pack_kernel(tg, pos_ref, a0, a1, a2, a3, a4, b0, b1, b2, b3, b4, pick_ref, out_ref):
    y = pos_ref[0]
    width = a0.shape[1]
    a_parts = (a0, a1, a2, (a3, a4))
    half = SIDE // 2
    for j, off in enumerate(OFFS):
        row = lax.rem(y + off, SIDE)
        if j < 3:
            a = a_parts[j][...]
        else:
            a = jnp.concatenate([a3[...], a4[...]], 0)
        step = a.shape[0] // SIDE
        a = jnp.concatenate([a[i * step : i * step + tg] for i in range(SIDE)], 0)
        far, at = (b3, j) if j < half else (b4, j - half)
        b = jnp.concatenate(
            [r[j * tg : (j + 1) * tg, :] for r in (b0, b1, b2)] + [far[at * tg : (at + 1) * tg, :]],
            0,
        )
        start = pl.multiple_of(row * BAND, 16)
        got_a = dot(pick_ref[row], a).astype(BF)
        got_b = dot(pick_ref[row], b).astype(BF)
        for e in range(2):
            out_ref[e, pl.ds(start, BAND), :width] = got_a[e * BAND : (e + 1) * BAND]
            out_ref[e, pl.ds(start, BAND), width:] = got_b[e * BAND : (e + 1) * BAND]


def pack_rows(pos, a_parts, b_parts, pick, blk, feats):
    tg = b_parts[0].shape[0] // SIDE
    specs = [pl.BlockSpec((p.shape[0], blk), lambda f, s: (0, f)) for p in a_parts + b_parts]
    return pl.pallas_call(
        functools.partial(pack_kernel, tg),
        out_shape=jax.ShapeDtypeStruct((2, ROWS, feats), BF),
        grid_spec=pltpu.PrefetchScalarGridSpec(
            num_scalar_prefetch=1,
            grid=(feats // (2 * blk),),
            in_specs=specs + [pl.BlockSpec(pick.shape, lambda f, s: (0, 0, 0))],
            out_specs=pl.BlockSpec((2, ROWS, 2 * blk), lambda f, s: (0, 0, f)),
        ),
        compiler_params=pltpu.CompilerParams(vmem_limit_bytes=56 * MIB),
        cost_estimate=pl.CostEstimate(
            flops=2 * 2 * ROWS * SIDE * tg * feats, transcendentals=0, bytes_accessed=14 * 2**20
        ),
        name="pack",
    )(pos, *a_parts, *b_parts, pick)


def pack_plain_kernel(rows_ref, pick_ref, out_ref):
    got = dot(pick_ref[0], rows_ref[...]).astype(BF)
    for e in range(2):
        out_ref[e] = got[e * BAND : (e + 1) * BAND]


def pack_plain(rows, pick, feats, blk=2048):
    depth = pick.shape[2]
    return pl.pallas_call(
        pack_plain_kernel,
        out_shape=jax.ShapeDtypeStruct((2, ROWS, feats), BF),
        grid=(SIDE, feats // blk),
        in_specs=[
            pl.BlockSpec((depth, blk), lambda y, f: (y, f)),
            pl.BlockSpec((1, 2 * BAND, depth), lambda y, f: (y, 0, 0)),
        ],
        out_specs=pl.BlockSpec((2, BAND, blk), lambda y, f: (0, y, f)),
        compiler_params=pltpu.CompilerParams(vmem_limit_bytes=56 * MIB),
        cost_estimate=pl.CostEstimate(
            flops=2 * 2 * ROWS * depth * feats, transcendentals=0, bytes_accessed=14 * 2**20
        ),
        name="pack_plain",
    )(rows, pick)


def own_at(n):
    return lambda e, j, s: (e, 0, jnp.minimum(j, n - 1))


def other_at(n):
    return lambda e, j, s: (e, 0, jnp.maximum(j - n, 0))


def col_at(n):
    def at(e, j, s):
        first = j < n
        core = jnp.where(first, s[1], 1 - s[1])
        return (e, 0, core * n + jnp.where(first, j, j - n))

    return at


def pre_kernel(core_ref, own, other, wg, wu, out, x_buf, w_buf, sems):
    core = core_ref[0]
    hid = wg.shape[1]
    feats = own.shape[2]
    lo = pl.multiple_of(core * feats, feats)
    hi = pl.multiple_of((1 - core) * feats, feats)
    copies = []
    for e in range(2):
        copies += [
            pltpu.make_async_copy(own.at[e], x_buf.at[e, :, pl.ds(lo, feats)], sems.at[4 * e]),
            pltpu.make_async_copy(wg.at[e], w_buf.at[e, pl.ds(0, hid)], sems.at[4 * e + 1]),
            pltpu.make_async_copy(wu.at[e], w_buf.at[e, pl.ds(hid, hid)], sems.at[4 * e + 2]),
            pltpu.make_async_copy(other.at[e], x_buf.at[e, :, pl.ds(hi, feats)], sems.at[4 * e + 3]),
        ]
    for c in copies:
        c.start()
    for e in range(2):
        for c in copies[4 * e : 4 * e + 4]:
            c.wait()
        out[e] = dot_t(x_buf[e], w_buf[e])


ANY = pl.BlockSpec(memory_space=pl.ANY)
IN_VMEM = pl.BlockSpec(memory_space=pltpu.VMEM)
IN_SMEM = pl.BlockSpec(memory_space=pltpu.SMEM)


def pre_rows(core, own, other, w_gate, w_up):
    hid, width = w_gate.shape[1:]
    return pl.pallas_call(
        pre_kernel,
        out_shape=jax.ShapeDtypeStruct((2, ROWS, 2 * hid), F32),
        in_specs=[IN_SMEM, ANY, ANY, ANY, ANY],
        out_specs=IN_VMEM,
        scratch_shapes=[
            pltpu.VMEM((2, ROWS, width), BF),
            pltpu.VMEM((2, 2 * hid, width), BF),
            pltpu.SemaphoreType.DMA((8,)),
        ],
        compiler_params=pltpu.CompilerParams(vmem_limit_bytes=56 * MIB),
        cost_estimate=pl.CostEstimate(
            flops=2 * 4 * ROWS * hid * width, transcendentals=0, bytes_accessed=18 * 2**20
        ),
        name="pre",
    )(core, own, other, w_gate, w_up)


def mid_kernel(
    core_ref, own, other, wd, wg, wu, pre, g_ref,
    dx_a, keep_b, send_b, both_t, hid_t, score,
    y_buf, d_buf, w_buf, dx_buf, sems, out_sems,
):
    core = core_ref[0]
    hid, width = wd.shape[1:]
    feats = own.shape[2]
    part = width // 8
    lo = pl.multiple_of(core * feats, feats)
    hi = pl.multiple_of((1 - core) * feats, feats)
    order = (1, 0)
    copies = {}
    for e in order:
        copies[e] = [
            pltpu.make_async_copy(wd.at[e], d_buf.at[e], sems.at[5 * e]),
            pltpu.make_async_copy(own.at[e], y_buf.at[e, :, pl.ds(lo, feats)], sems.at[5 * e + 1]),
            pltpu.make_async_copy(other.at[e], y_buf.at[e, :, pl.ds(hi, feats)], sems.at[5 * e + 2]),
            pltpu.make_async_copy(wg.at[e], w_buf.at[e, pl.ds(0, hid)], sems.at[5 * e + 3]),
            pltpu.make_async_copy(wu.at[e], w_buf.at[e, pl.ds(hid, hid)], sems.at[5 * e + 4]),
        ]
        for c in copies[e]:
            c.start()
    ends = []
    for e in order:
        for c in copies[e][:3]:
            c.wait()
        dy = dot_t(y_buf[e], d_buf[e])
        gate, up, g = pre[e, :, :hid], pre[e, :, hid:], g_ref[e]
        s = jax.nn.sigmoid(gate)
        act = gate * s
        hidden = act * up
        score[e] = jnp.sum(hidden * dy, axis=1, keepdims=True)
        d_hid = dy * g
        d_up = d_hid * act
        d_gate = d_hid * up * s * (1.0 + gate * (1.0 - s))
        both = jnp.concatenate([d_gate, d_up], 1)
        both_t[e] = both.T.astype(BF)
        hid_t[e] = (hidden * g).T.astype(BF)
        for c in copies[e][3:]:
            c.wait()
        if e == 0:
            left = both.astype(BF)
            for k in range(4):
                cols = pl.ds(k * 2 * part, 2 * part)
                dx_buf[e, pl.ds(0, ROWS), cols] = dot(left, w_buf[e, :, cols]).astype(BF)
                c = pltpu.make_async_copy(
                    dx_buf.at[e, pl.ds(0, ROWS), cols], dx_a.at[:, cols], out_sems.at[8 + k]
                )
                c.start()
                ends.append(c)
        else:
            gap = jnp.zeros((PAD - CAP, 2 * hid), F32)
            rows = []
            for i in range(SIDE * SIDE):
                rows += [both[i * CAP : (i + 1) * CAP], gap]
            left = jnp.concatenate(rows, 0).astype(BF)
            for k in range(8):
                cols = pl.ds(k * part, part)
                to = pl.ds(k // 2 * part, part)
                dx_buf[e, :, cols] = dot(left, w_buf[e, :, cols]).astype(BF)
                kept = pltpu.make_async_copy(dx_buf.at[e, :, cols], keep_b.at[:, to], out_sems.at[k])
                sent = pltpu.make_async_copy(dx_buf.at[e, :, cols], send_b.at[:, to], out_sems.at[k])

                @pl.when(core == k % 2)
                def _():
                    kept.start()

                @pl.when(core != k % 2)
                def _():
                    sent.start()

                ends.append(kept)
    for c in ends:
        c.wait()


def mid_rows(core, own, other, w_down, w_gate, w_up, pre, g):
    hid, width = w_down.shape[1:]
    tall = SIDE * SIDE * PAD
    return pl.pallas_call(
        mid_kernel,
        out_shape=[
            jax.ShapeDtypeStruct((ROWS, width), BF),
            jax.ShapeDtypeStruct((tall, width // 2), BF),
            jax.ShapeDtypeStruct((tall, width // 2), BF),
            jax.ShapeDtypeStruct((2, 2 * hid, ROWS), BF),
            jax.ShapeDtypeStruct((2, hid, ROWS), BF),
            jax.ShapeDtypeStruct((2, ROWS, 1), F32),
        ],
        in_specs=[IN_SMEM, ANY, ANY, ANY, ANY, ANY, IN_VMEM, IN_VMEM],
        out_specs=[ANY, ANY, ANY, IN_VMEM, IN_VMEM, IN_VMEM],
        scratch_shapes=[
            pltpu.VMEM((2, ROWS, width), BF),
            pltpu.VMEM((2, hid, width), BF),
            pltpu.VMEM((2, 2 * hid, width), BF),
            pltpu.VMEM((2, tall, width), BF),
            pltpu.SemaphoreType.DMA((10,)),
            pltpu.SemaphoreType.DMA((12,)),
        ],
        compiler_params=pltpu.CompilerParams(vmem_limit_bytes=56 * MIB),
        cost_estimate=pl.CostEstimate(
            flops=2 * 6 * ROWS * hid * width,
            transcendentals=2 * ROWS * hid,
            bytes_accessed=34 * 2**20,
        ),
        name="mid",
    )(core, own, other, w_down, w_gate, w_up, pre, g)


def grad_kernel(n, pos_ref, x_own, x_other, y_own, y_other, both_t, hid_t, gg, gu, gd):
    j = pl.program_id(1)
    hid = gg.shape[1]

    def put(x, y):
        r = dot(both_t[0], x)
        gg[0] = r[:hid].astype(BF)
        gu[0] = r[hid:].astype(BF)
        gd[0] = dot(hid_t[0], y).astype(BF)

    @pl.when(j < n)
    def _():
        put(x_own[0], y_own[0])

    @pl.when(j >= n)
    def _():
        put(x_other[0], y_other[0])


def grad_rows(pos, x_own, x_other, y_own, y_other, both_t, hid_t, blk=1024):
    hid = hid_t.shape[1]
    n = x_own.shape[2] // blk
    whole = lambda e, j, s: (e, 0, 0)
    return pl.pallas_call(
        functools.partial(grad_kernel, n),
        out_shape=[jax.ShapeDtypeStruct((2, hid, 2 * n * blk), BF)] * 3,
        grid_spec=pltpu.PrefetchScalarGridSpec(
            num_scalar_prefetch=1,
            grid=(2, 2 * n),
            in_specs=[
                pl.BlockSpec((1, ROWS, blk), own_at(n)),
                pl.BlockSpec((1, ROWS, blk), other_at(n)),
                pl.BlockSpec((1, ROWS, blk), own_at(n)),
                pl.BlockSpec((1, ROWS, blk), other_at(n)),
                pl.BlockSpec((1, 2 * hid, ROWS), whole),
                pl.BlockSpec((1, hid, ROWS), whole),
            ],
            out_specs=[pl.BlockSpec((1, hid, blk), col_at(n))] * 3,
        ),
        compiler_params=pltpu.CompilerParams(vmem_limit_bytes=56 * MIB),
        cost_estimate=pl.CostEstimate(
            flops=2 * 6 * ROWS * hid * n * 2 * blk, transcendentals=0, bytes_accessed=30 * 2**20
        ),
        name="grads",
    )(pos, x_own, x_other, y_own, y_other, both_t, hid_t)


def before_count(member):
    t = member.shape[-1]
    upper = (jnp.arange(t)[:, None] < jnp.arange(t)[None, :]).astype(BF)
    return jnp.dot(member.astype(BF), upper, preferred_element_type=F32).astype(jnp.int32)


def on_device(tokens, cotangent, gate_values, expert_ids, w_gate, w_up, w_down):
    tg, top = expert_ids.shape
    width = tokens.shape[1]
    n_exp = lax.axis_size("expert")
    experts = 2 * n_exp
    me = lax.axis_index("expert")
    lane = lax.axis_index("tensor")
    y, z, core = me // SIDE, me % SIDE, lane % 2
    pos = jnp.stack([y, core]).astype(jnp.int32)
    feats = width // 2
    blk = 256

    def half(v):
        return lax.dynamic_slice_in_dim(v, core * feats, feats, 1)

    route = jnp.concatenate([expert_ids.astype(BF), gate_values], 1)
    route = jnp.pad(route, ((0, 0), (0, 128 - 2 * top)))
    x_all = lax.all_gather(
        jnp.concatenate([half(tokens), route], 1), "expert", axis=0, tiled=True
    )
    y_half = half(cotangent).reshape(tg, feats // (2 * blk), 2, blk)
    ya = y_half[:, :, 0].reshape(tg, feats // 2)
    yb = y_half[:, :, 1].reshape(tg, feats // 2)
    ya1 = jnp.concatenate(ring(ya, "z"), 0)
    yb1 = jnp.concatenate(ring(yb, "y"), 0)
    ya_parts, yb_parts = ring(ya1, "y"), ring(yb1, "z")

    x_all = after_all(x_all, (ya_parts, yb_parts))

    tab = x_all[:, feats : feats + 2 * top].reshape(SIDE, SIDE, tg, 2 * top)
    ids = tab[..., :top].astype(jnp.int32)
    gates = tab[..., top:].astype(F32)
    mine = 2 * me + jnp.arange(2)
    named = ids[None] == mine[:, None, None, None, None]
    member = jnp.any(named, -1)
    weight = jnp.sum(jnp.where(named, gates[None], 0.0), -1)
    count = before_count(member)
    target = jnp.where(member, jnp.arange(SIDE)[None, None, :, None] * CAP + count, -1)

    def hits(v):
        return v.reshape(2, SIDE, 1, SIDE * tg) == jnp.arange(BAND)[None, None, :, None]

    def picks(v):
        return hits(v).astype(BF).transpose(1, 0, 2, 3).reshape(SIDE, 2 * BAND, SIDE * tg)

    pick = picks(target)
    pick_ring = picks(target[:, :, (z + jnp.array(OFFS)) % SIDE])
    g_slot = jnp.sum(jnp.where(hits(target), weight.reshape(2, SIDE, 1, SIDE * tg), 0.0), -1)
    g_slot = g_slot.reshape(2, ROWS, 1)

    x_own = pack_plain(x_all, pick, feats)
    x_other = swap_core(x_own)
    y_own = pack_rows(pos, ya_parts, yb_parts, pick_ring, blk, feats)
    cores = core.astype(jnp.int32).reshape(1)
    pre = pre_rows(cores, x_own, x_other, w_gate, w_up)
    y_other = swap_core(y_own)
    dx_a, keep_b, send_b, both_t, hid_t, score = mid_rows(
        cores, y_own, y_other, w_down, w_gate, w_up, pre, g_slot
    )

    n_ten = lax.axis_size("tensor")
    part = width // n_ten
    share = lax.psum_scatter(dx_a, "tensor", scatter_dimension=1, tiled=True)
    came = swap_core(send_b)
    out_b = (keep_b.astype(F32) + came.astype(F32)).astype(BF)
    back_b = lax.all_to_all(out_b, "expert", split_axis=0, concat_axis=0, tiled=True)
    both_t, hid_t = after_all((both_t, hid_t), out_b)
    grads = grad_rows(pos, x_own, x_other, y_own, y_other, both_t, hid_t)

    total = score.reshape(ROWS * 2 // 128, 128)
    for bit in (1, 2, 4):
        total = total + lax.ppermute(total, "tensor", [(i, i ^ bit) for i in range(n_ten)])

    own_named = expert_ids[:, :, None] == jnp.arange(experts)[None, None, :]
    own_member = jnp.any(own_named, 1)
    own_count = before_count(own_member.T).T
    own_hit = own_member[:, :, None] & (own_count[:, :, None] == jnp.arange(PAD)[None, None, :])
    spread = own_hit.astype(BF).reshape(tg, n_exp, 2, PAD)
    spread_a, spread_b = spread[:, :, 0], spread[:, :, 1]

    grads, back_b = lax.optimization_barrier((grads, back_b))
    sum_b = jnp.einsum(
        "tns,nsf->tf",
        spread_b,
        back_b.reshape(n_exp, PAD, width // 2),
        preferred_element_type=F32,
    ).astype(BF)
    x = lane // 2
    mine_b = lax.dynamic_slice_in_dim(sum_b, x * part, part, 1).astype(F32)
    for step in range(1, n_ten // 2):
        piece = lax.dynamic_slice_in_dim(sum_b, (x + step) % (n_ten // 2) * part, part, 1)
        perm = [(i, (i + 2 * step) % n_ten) for i in range(n_ten)]
        mine_b = mine_b + lax.ppermute(piece, "tensor", perm).astype(F32)

    back = jnp.pad(share.reshape(n_exp, CAP, part), ((0, 0), (0, PAD - CAP), (0, 0)))
    line = total.reshape(2, n_exp, CAP).transpose(1, 0, 2).reshape(n_exp, 1, 2 * CAP).astype(BF)
    line = jnp.pad(line, ((0, 0), (0, 7), (0, part - 2 * CAP)))
    back = jnp.concatenate([back, line], 1)
    back = after_all(back, (mine_b, spread_a, own_hit, own_named))
    back = lax.all_to_all(back, "expert", split_axis=0, concat_axis=0, tiled=True)
    sum_a = jnp.einsum("tns,nsf->tf", spread_a, back[:, :PAD], preferred_element_type=F32)
    d_tokens = (sum_a + mine_b).astype(BF)
    scores = back[:, PAD, : 2 * CAP].reshape(experts, CAP).astype(F32)
    by_expert = jnp.sum(jnp.where(own_hit[:, :, :CAP], scores[None], 0.0), 2)
    d_gates = jnp.sum(jnp.where(own_named, by_expert[:, None, :], 0.0), 2).astype(BF)
    return (d_tokens, d_gates) + tuple(grads)


def solution(mesh):
    placed = (
        P("expert", None),
        P("expert", None),
        P("expert", None),
        P("expert", None),
        P("expert", "tensor", None),
        P("expert", "tensor", None),
        P("expert", "tensor", None),
    )
    return jax.shard_map(
        on_device,
        mesh=mesh,
        in_specs=placed,
        out_specs=(
            P("expert", "tensor"),
            P("expert", None),
            P("expert", "tensor", None),
            P("expert", "tensor", None),
            P("expert", "tensor", None),
        ),
        check_vma=False,
    )
```

```python
import functools

import jax
import jax.numpy as jnp
from jax import lax
from jax.experimental import pallas as pl
from jax.experimental.pallas import tpu as pltpu
from jax.sharding import PartitionSpec as P

BF = jnp.bfloat16
F32 = jnp.float32
SIDE = 4
OFFS = (0, 3, 1, 2)
CAP = 36
ROWS = SIDE * SIDE * CAP
BAND = SIDE * CAP
PAD = 40
MIB = 1024 * 1024


def dot(a, b):
    return lax.dot_general(a, b, (((1,), (0,)), ((), ())), preferred_element_type=F32)


def dot_t(a, b):
    return lax.dot_general(a, b, (((1,), (1,)), ((), ())), preferred_element_type=F32)


def t_dot(a, b):
    return lax.dot_general(a, b, (((0,), (0,)), ((), ())), preferred_element_type=F32)


def shift(v, axis, step):
    perm = []
    for y in range(SIDE):
        for z in range(SIDE):
            to = ((y + step) % SIDE, z) if axis == "y" else (y, (z + step) % SIDE)
            perm.append((y * SIDE + z, to[0] * SIDE + to[1]))
    return lax.ppermute(v, "expert", perm)


def swap_core(v):
    n = lax.axis_size("tensor")
    return lax.ppermute(v, "tensor", [(i, i ^ 1) for i in range(n)])


def near(v, axis):
    return (v, shift(v, axis, 1), shift(v, axis, -1))


def far(blocks, axis, half=None):
    v, before, after = blocks
    half = half or v.shape[0] // 2
    return (shift(before[:half], axis, 1), shift(after[half:], axis, -1))


def ring(v, axis, half=None):
    blocks = near(v, axis)
    return blocks + far(blocks, axis, half)


def after_all(values, others):
    return lax.optimization_barrier((values, others))[0]


def pack_kernel(tg, pos_ref, a0, a1, a2, a3, a4, b0, b1, b2, b3, b4, pick_ref, out_ref):
    y = pos_ref[0]
    width = a0.shape[1]
    a_parts = (a0, a1, a2, (a3, a4))
    half = SIDE // 2
    for j, off in enumerate(OFFS):
        row = lax.rem(y + off, SIDE)
        if j < 3:
            a = a_parts[j][...]
        else:
            a = jnp.concatenate([a3[...], a4[...]], 0)
        step = a.shape[0] // SIDE
        a = jnp.concatenate([a[i * step : i * step + tg] for i in range(SIDE)], 0)
        far, at = (b3, j) if j < half else (b4, j - half)
        b = jnp.concatenate(
            [r[j * tg : (j + 1) * tg, :] for r in (b0, b1, b2)] + [far[at * tg : (at + 1) * tg, :]],
            0,
        )
        start = pl.multiple_of(row * BAND, 16)
        got_a = dot(pick_ref[row], a).astype(BF)
        got_b = dot(pick_ref[row], b).astype(BF)
        for e in range(2):
            out_ref[e, pl.ds(start, BAND), :width] = got_a[e * BAND : (e + 1) * BAND]
            out_ref[e, pl.ds(start, BAND), width:] = got_b[e * BAND : (e + 1) * BAND]


def pack_rows(pos, a_parts, b_parts, pick, blk, feats):
    tg = b_parts[0].shape[0] // SIDE
    specs = [pl.BlockSpec((p.shape[0], blk), lambda f, s: (0, f)) for p in a_parts + b_parts]
    return pl.pallas_call(
        functools.partial(pack_kernel, tg),
        out_shape=jax.ShapeDtypeStruct((2, ROWS, feats), BF),
        grid_spec=pltpu.PrefetchScalarGridSpec(
            num_scalar_prefetch=1,
            grid=(feats // (2 * blk),),
            in_specs=specs + [pl.BlockSpec(pick.shape, lambda f, s: (0, 0, 0))],
            out_specs=pl.BlockSpec((2, ROWS, 2 * blk), lambda f, s: (0, 0, f)),
        ),
        compiler_params=pltpu.CompilerParams(vmem_limit_bytes=56 * MIB),
        cost_estimate=pl.CostEstimate(
            flops=2 * 2 * ROWS * SIDE * tg * feats, transcendentals=0, bytes_accessed=14 * 2**20
        ),
        name="pack",
    )(pos, *a_parts, *b_parts, pick)


def pack_plain_kernel(rows_ref, pick_ref, out_ref):
    got = dot(pick_ref[0], rows_ref[...]).astype(BF)
    for e in range(2):
        out_ref[e] = got[e * BAND : (e + 1) * BAND]


def pack_plain(rows, pick, feats, blk=2048):
    depth = pick.shape[2]
    return pl.pallas_call(
        pack_plain_kernel,
        out_shape=jax.ShapeDtypeStruct((2, ROWS, feats), BF),
        grid=(SIDE, feats // blk),
        in_specs=[
            pl.BlockSpec((depth, blk), lambda y, f: (y, f)),
            pl.BlockSpec((1, 2 * BAND, depth), lambda y, f: (y, 0, 0)),
        ],
        out_specs=pl.BlockSpec((2, BAND, blk), lambda y, f: (0, y, f)),
        compiler_params=pltpu.CompilerParams(vmem_limit_bytes=56 * MIB),
        cost_estimate=pl.CostEstimate(
            flops=2 * 2 * ROWS * depth * feats, transcendentals=0, bytes_accessed=14 * 2**20
        ),
        name="pack_plain",
    )(rows, pick)


def own_at(n):
    return lambda e, j, s: (e, 0, jnp.minimum(j, n - 1))


def other_at(n):
    return lambda e, j, s: (e, 0, jnp.maximum(j - n, 0))


def col_at(n):
    def at(e, j, s):
        first = j < n
        core = jnp.where(first, s[1], 1 - s[1])
        return (e, 0, core * n + jnp.where(first, j, j - n))

    return at


def pre_kernel(core_ref, own, other, wg, wu, out, x_buf, w_buf, sems):
    core = core_ref[0]
    hid = wg.shape[1]
    feats = own.shape[2]
    lo = pl.multiple_of(core * feats, feats)
    hi = pl.multiple_of((1 - core) * feats, feats)
    copies = []
    for e in range(2):
        copies += [
            pltpu.make_async_copy(own.at[e], x_buf.at[e, :, pl.ds(lo, feats)], sems.at[4 * e]),
            pltpu.make_async_copy(wg.at[e], w_buf.at[e, pl.ds(0, hid)], sems.at[4 * e + 1]),
            pltpu.make_async_copy(wu.at[e], w_buf.at[e, pl.ds(hid, hid)], sems.at[4 * e + 2]),
            pltpu.make_async_copy(other.at[e], x_buf.at[e, :, pl.ds(hi, feats)], sems.at[4 * e + 3]),
        ]
    for c in copies:
        c.start()
    for e in range(2):
        for c in copies[4 * e : 4 * e + 4]:
            c.wait()
        out[e] = dot_t(x_buf[e], w_buf[e])


ANY = pl.BlockSpec(memory_space=pl.ANY)
IN_VMEM = pl.BlockSpec(memory_space=pltpu.VMEM)
IN_SMEM = pl.BlockSpec(memory_space=pltpu.SMEM)


def pre_rows(core, own, other, w_gate, w_up):
    hid, width = w_gate.shape[1:]
    return pl.pallas_call(
        pre_kernel,
        out_shape=jax.ShapeDtypeStruct((2, ROWS, 2 * hid), F32),
        in_specs=[IN_SMEM, ANY, ANY, ANY, ANY],
        out_specs=IN_VMEM,
        scratch_shapes=[
            pltpu.VMEM((2, ROWS, width), BF),
            pltpu.VMEM((2, 2 * hid, width), BF),
            pltpu.SemaphoreType.DMA((8,)),
        ],
        compiler_params=pltpu.CompilerParams(vmem_limit_bytes=56 * MIB),
        cost_estimate=pl.CostEstimate(
            flops=2 * 4 * ROWS * hid * width, transcendentals=0, bytes_accessed=18 * 2**20
        ),
        name="pre",
    )(core, own, other, w_gate, w_up)


def mid_kernel(
    core_ref, own, other, wd, wg, wu, pre, g_ref,
    dx_a, keep_b, send_b, both_o, hid_o, score,
    y_buf, d_buf, w_buf, dx_buf, sems, out_sems,
):
    core = core_ref[0]
    hid, width = wd.shape[1:]
    feats = own.shape[2]
    part = width // 8
    lo = pl.multiple_of(core * feats, feats)
    hi = pl.multiple_of((1 - core) * feats, feats)
    order = (1, 0)
    copies = {}
    for e in order:
        copies[e] = [
            pltpu.make_async_copy(wd.at[e], d_buf.at[e], sems.at[5 * e]),
            pltpu.make_async_copy(own.at[e], y_buf.at[e, :, pl.ds(lo, feats)], sems.at[5 * e + 1]),
            pltpu.make_async_copy(other.at[e], y_buf.at[e, :, pl.ds(hi, feats)], sems.at[5 * e + 2]),
            pltpu.make_async_copy(wg.at[e], w_buf.at[e, pl.ds(0, hid)], sems.at[5 * e + 3]),
            pltpu.make_async_copy(wu.at[e], w_buf.at[e, pl.ds(hid, hid)], sems.at[5 * e + 4]),
        ]
    for c in copies[order[0]]:
        c.start()
    ends = []
    for e in order:
        gate, up, g = pre[e, :, :hid], pre[e, :, hid:], g_ref[e]
        s = jax.nn.sigmoid(gate)
        act = gate * s
        hidden = act * up
        slope = up * s * (1.0 + gate * (1.0 - s))
        hid_o[e] = (hidden * g).astype(BF)
        for c in copies[e][:3]:
            c.wait()
        if e == order[0]:
            for c in copies[order[1]]:
                c.start()
        dy = dot_t(y_buf[e], d_buf[e])
        score[e] = jnp.sum(hidden * dy, axis=1, keepdims=True)
        d_hid = dy * g
        both = jnp.concatenate([d_hid * slope, d_hid * act], 1)
        both_o[e] = both.astype(BF)
        for c in copies[e][3:]:
            c.wait()
        if e == 0:
            left = both.astype(BF)
            for k in range(4):
                cols = pl.ds(k * 2 * part, 2 * part)
                dx_buf[e, pl.ds(0, ROWS), cols] = dot(left, w_buf[e, :, cols]).astype(BF)
                c = pltpu.make_async_copy(
                    dx_buf.at[e, pl.ds(0, ROWS), cols], dx_a.at[:, cols], out_sems.at[8 + k]
                )
                c.start()
                ends.append(c)
        else:
            gap = jnp.zeros((PAD - CAP, 2 * hid), F32)
            rows = []
            for i in range(SIDE * SIDE):
                rows += [both[i * CAP : (i + 1) * CAP], gap]
            left = jnp.concatenate(rows, 0).astype(BF)
            for k in range(8):
                cols = pl.ds(k * part, part)
                to = pl.ds(k // 2 * part, part)
                dx_buf[e, :, cols] = dot(left, w_buf[e, :, cols]).astype(BF)
                kept = pltpu.make_async_copy(dx_buf.at[e, :, cols], keep_b.at[:, to], out_sems.at[k])
                sent = pltpu.make_async_copy(dx_buf.at[e, :, cols], send_b.at[:, to], out_sems.at[k])

                @pl.when(core == k % 2)
                def _():
                    kept.start()

                @pl.when(core != k % 2)
                def _():
                    sent.start()

                ends.append(kept)
    for c in ends:
        c.wait()


def mid_rows(core, own, other, w_down, w_gate, w_up, pre, g):
    hid, width = w_down.shape[1:]
    tall = SIDE * SIDE * PAD
    return pl.pallas_call(
        mid_kernel,
        out_shape=[
            jax.ShapeDtypeStruct((ROWS, width), BF),
            jax.ShapeDtypeStruct((tall, width // 2), BF),
            jax.ShapeDtypeStruct((tall, width // 2), BF),
            jax.ShapeDtypeStruct((2, ROWS, 2 * hid), BF),
            jax.ShapeDtypeStruct((2, ROWS, hid), BF),
            jax.ShapeDtypeStruct((2, ROWS, 1), F32),
        ],
        in_specs=[IN_SMEM, ANY, ANY, ANY, ANY, ANY, IN_VMEM, IN_VMEM],
        out_specs=[ANY, ANY, ANY, IN_VMEM, IN_VMEM, IN_VMEM],
        scratch_shapes=[
            pltpu.VMEM((2, ROWS, width), BF),
            pltpu.VMEM((2, hid, width), BF),
            pltpu.VMEM((2, 2 * hid, width), BF),
            pltpu.VMEM((2, tall, width), BF),
            pltpu.SemaphoreType.DMA((10,)),
            pltpu.SemaphoreType.DMA((12,)),
        ],
        compiler_params=pltpu.CompilerParams(vmem_limit_bytes=56 * MIB),
        cost_estimate=pl.CostEstimate(
            flops=2 * 6 * ROWS * hid * width,
            transcendentals=2 * ROWS * hid,
            bytes_accessed=34 * 2**20,
        ),
        name="mid",
    )(core, own, other, w_down, w_gate, w_up, pre, g)


def grad_kernel(n, pos_ref, x_own, x_other, y_own, y_other, both_o, hid_o, gg, gu, gd):
    j = pl.program_id(1)
    hid = gg.shape[1]

    def put(x, y):
        r = t_dot(both_o[0], x)
        gg[0] = r[:hid].astype(BF)
        gu[0] = r[hid:].astype(BF)
        gd[0] = t_dot(hid_o[0], y).astype(BF)

    @pl.when(j < n)
    def _():
        put(x_own[0], y_own[0])

    @pl.when(j >= n)
    def _():
        put(x_other[0], y_other[0])


def grad_rows(pos, x_own, x_other, y_own, y_other, both_o, hid_o, blk=1024):
    hid = hid_o.shape[2]
    n = x_own.shape[2] // blk
    whole = lambda e, j, s: (e, 0, 0)
    return pl.pallas_call(
        functools.partial(grad_kernel, n),
        out_shape=[jax.ShapeDtypeStruct((2, hid, 2 * n * blk), BF)] * 3,
        grid_spec=pltpu.PrefetchScalarGridSpec(
            num_scalar_prefetch=1,
            grid=(2, 2 * n),
            in_specs=[
                pl.BlockSpec((1, ROWS, blk), own_at(n)),
                pl.BlockSpec((1, ROWS, blk), other_at(n)),
                pl.BlockSpec((1, ROWS, blk), own_at(n)),
                pl.BlockSpec((1, ROWS, blk), other_at(n)),
                pl.BlockSpec((1, ROWS, 2 * hid), whole),
                pl.BlockSpec((1, ROWS, hid), whole),
            ],
            out_specs=[pl.BlockSpec((1, hid, blk), col_at(n))] * 3,
        ),
        compiler_params=pltpu.CompilerParams(vmem_limit_bytes=56 * MIB),
        cost_estimate=pl.CostEstimate(
            flops=2 * 6 * ROWS * hid * n * 2 * blk, transcendentals=0, bytes_accessed=30 * 2**20
        ),
        name="grads",
    )(pos, x_own, x_other, y_own, y_other, both_o, hid_o)


def before_count(member):
    t = member.shape[-1]
    upper = (jnp.arange(t)[:, None] < jnp.arange(t)[None, :]).astype(BF)
    return jnp.dot(member.astype(BF), upper, preferred_element_type=F32).astype(jnp.int32)


def on_device(tokens, cotangent, gate_values, expert_ids, w_gate, w_up, w_down):
    tg, top = expert_ids.shape
    width = tokens.shape[1]
    n_exp = lax.axis_size("expert")
    experts = 2 * n_exp
    me = lax.axis_index("expert")
    lane = lax.axis_index("tensor")
    y, z, core = me // SIDE, me % SIDE, lane % 2
    pos = jnp.stack([y, core]).astype(jnp.int32)
    feats = width // 2
    blk = 512

    def half(v):
        return lax.dynamic_slice_in_dim(v, core * feats, feats, 1)

    x_all = lax.all_gather(half(tokens), "expert", axis=0, tiled=True)
    y_half = half(cotangent).reshape(tg, feats // (2 * blk), 2, blk)
    ya = y_half[:, :, 0].reshape(tg, feats // 2)
    yb = y_half[:, :, 1].reshape(tg, feats // 2)
    ya1 = jnp.concatenate(ring(ya, "z"), 0)
    yb1 = jnp.concatenate(ring(yb, "y"), 0)

    route = jnp.concatenate([expert_ids.astype(BF), gate_values], 1)
    route = route.reshape(2 * tg * top // 128, 128)
    route = after_all(jnp.tile(route, (n_exp, 1)), (ya1, yb1))
    route = lax.all_to_all(route, "expert", split_axis=0, concat_axis=0, tiled=True)
    tab = route.reshape(SIDE, SIDE, tg, 2 * top)
    ids = tab[..., :top].astype(jnp.int32)
    gates = tab[..., top:].astype(F32)
    mine = 2 * me + jnp.arange(2)
    named = ids[None] == mine[:, None, None, None, None]
    member = jnp.any(named, -1)
    weight = jnp.sum(jnp.where(named, gates[None], 0.0), -1)
    count = before_count(member)
    target = jnp.where(member, jnp.arange(SIDE)[None, None, :, None] * CAP + count, -1)

    def hits(v):
        return v.reshape(2, SIDE, 1, SIDE * tg) == jnp.arange(BAND)[None, None, :, None]

    def picks(v):
        return hits(v).astype(BF).transpose(1, 0, 2, 3).reshape(SIDE, 2 * BAND, SIDE * tg)

    pick = picks(target)
    pick_ring = picks(target[:, :, (z + jnp.array(OFFS)) % SIDE])
    g_slot = jnp.sum(jnp.where(hits(target), weight.reshape(2, SIDE, 1, SIDE * tg), 0.0), -1)
    g_slot = g_slot.reshape(2, ROWS, 1)

    ya_parts, yb_parts = near(ya1, "y"), near(yb1, "z")
    ya_parts, yb_parts, pick, pick_ring, g_slot = lax.optimization_barrier(
        (ya_parts, yb_parts, pick, pick_ring, g_slot)
    )
    ya_parts, yb_parts = ya_parts + far(ya_parts, "y"), yb_parts + far(yb_parts, "z")
    x_all = after_all(x_all, (ya_parts, yb_parts))

    x_own = pack_plain(x_all, pick, feats)
    x_other = swap_core(x_own)
    y_own = pack_rows(pos, ya_parts, yb_parts, pick_ring, blk, feats)
    pre = pre_rows(core.astype(jnp.int32).reshape(1), x_own, x_other, w_gate, w_up)
    cores = core.astype(jnp.int32).reshape(1)
    y_other = swap_core(y_own)
    dx_a, keep_b, send_b, both_o, hid_o, score = mid_rows(
        cores, y_own, y_other, w_down, w_gate, w_up, pre, g_slot
    )

    n_ten = lax.axis_size("tensor")
    part = width // n_ten
    share = lax.psum_scatter(dx_a, "tensor", scatter_dimension=1, tiled=True)
    came = swap_core(send_b)
    out_b = (keep_b.astype(F32) + came.astype(F32)).astype(BF)
    back_b = lax.all_to_all(out_b, "expert", split_axis=0, concat_axis=0, tiled=True)
    both_o, hid_o = after_all((both_o, hid_o), out_b)
    grads = grad_rows(pos, x_own, x_other, y_own, y_other, both_o, hid_o)

    total = score.reshape(ROWS * 2 // 128, 128)
    for bit in (1, 2, 4):
        total = total + lax.ppermute(total, "tensor", [(i, i ^ bit) for i in range(n_ten)])

    own_named = expert_ids[:, :, None] == jnp.arange(experts)[None, None, :]
    own_member = jnp.any(own_named, 1)
    own_count = before_count(own_member.T).T
    own_hit = own_member[:, :, None] & (own_count[:, :, None] == jnp.arange(PAD)[None, None, :])
    spread = own_hit.astype(BF).reshape(tg, n_exp, 2, PAD)
    spread_a, spread_b = spread[:, :, 0], spread[:, :, 1]

    back = jnp.pad(share.reshape(n_exp, CAP, part), ((0, 0), (0, PAD - CAP), (0, 0)))
    line = total.reshape(2, n_exp, CAP).transpose(1, 0, 2).reshape(n_exp, 1, 2 * CAP).astype(BF)
    line = jnp.pad(line, ((0, 0), (0, 7), (0, part - 2 * CAP)))
    back = jnp.concatenate([back, line], 1)
    back, grads = lax.optimization_barrier((back, grads))
    back = lax.all_to_all(back, "expert", split_axis=0, concat_axis=0, tiled=True)
    sum_b = jnp.einsum(
        "tns,nsf->tf",
        spread_b,
        back_b.reshape(n_exp, PAD, width // 2),
        preferred_element_type=F32,
    ).astype(BF)
    x = lane // 2
    mine_b = lax.dynamic_slice_in_dim(sum_b, x * part, part, 1).astype(F32)
    for step in range(1, n_ten // 2):
        piece = lax.dynamic_slice_in_dim(sum_b, (x + step) % (n_ten // 2) * part, part, 1)
        perm = [(i, (i + 2 * step) % n_ten) for i in range(n_ten)]
        mine_b = mine_b + lax.ppermute(piece, "tensor", perm).astype(F32)

    sum_a = jnp.einsum("tns,nsf->tf", spread_a, back[:, :PAD], preferred_element_type=F32)
    d_tokens = (sum_a + mine_b).astype(BF)
    scores = back[:, PAD, : 2 * CAP].reshape(experts, CAP).astype(F32)
    by_expert = jnp.sum(jnp.where(own_hit[:, :, :CAP], scores[None], 0.0), 2)
    d_gates = jnp.sum(jnp.where(own_named, by_expert[:, None, :], 0.0), 2).astype(BF)
    return (d_tokens, d_gates) + tuple(grads)


def solution(mesh):
    placed = (
        P("expert", None),
        P("expert", None),
        P("expert", None),
        P("expert", None),
        P("expert", "tensor", None),
        P("expert", "tensor", None),
        P("expert", "tensor", None),
    )
    return jax.shard_map(
        on_device,
        mesh=mesh,
        in_specs=placed,
        out_specs=(
            P("expert", "tensor"),
            P("expert", None),
            P("expert", "tensor", None),
            P("expert", "tensor", None),
            P("expert", "tensor", None),
        ),
        check_vma=False,
    )
```

```python
import functools

import jax
import jax.numpy as jnp
from jax import lax
from jax.experimental import pallas as pl
from jax.experimental.pallas import tpu as pltpu
from jax.sharding import PartitionSpec as P

BF = jnp.bfloat16
F32 = jnp.float32
SIDE = 4
OFFS = (0, 3, 1, 2)
CAP = 36
ROWS = SIDE * SIDE * CAP
BAND = SIDE * CAP
PAD = 40
MIB = 1024 * 1024


def dot(a, b):
    return lax.dot_general(a, b, (((1,), (0,)), ((), ())), preferred_element_type=F32)


def dot_t(a, b):
    return lax.dot_general(a, b, (((1,), (1,)), ((), ())), preferred_element_type=F32)


def t_dot(a, b):
    return lax.dot_general(a, b, (((0,), (0,)), ((), ())), preferred_element_type=F32)


def shift(v, axis, step):
    perm = []
    for y in range(SIDE):
        for z in range(SIDE):
            to = ((y + step) % SIDE, z) if axis == "y" else (y, (z + step) % SIDE)
            perm.append((y * SIDE + z, to[0] * SIDE + to[1]))
    return lax.ppermute(v, "expert", perm)


def swap_core(v):
    n = lax.axis_size("tensor")
    return lax.ppermute(v, "tensor", [(i, i ^ 1) for i in range(n)])


def near(v, axis):
    return (v, shift(v, axis, 1), shift(v, axis, -1))


def far(blocks, axis, half=None):
    v, before, after = blocks
    half = half or v.shape[0] // 2
    return (shift(before[:half], axis, 1), shift(after[half:], axis, -1))


def ring(v, axis, half=None):
    blocks = near(v, axis)
    return blocks + far(blocks, axis, half)


def after_all(values, others):
    return lax.optimization_barrier((values, others))[0]


def pack_kernel(tg, pos_ref, a0, a1, a2, a3, a4, b0, b1, b2, b3, b4, pick_ref, out_ref):
    y = pos_ref[0]
    width = a0.shape[1]
    a_parts = (a0, a1, a2, (a3, a4))
    half = SIDE // 2
    for j, off in enumerate(OFFS):
        row = lax.rem(y + off, SIDE)
        if j < 3:
            a = a_parts[j][...]
        else:
            a = jnp.concatenate([a3[...], a4[...]], 0)
        step = a.shape[0] // SIDE
        a = jnp.concatenate([a[i * step : i * step + tg] for i in range(SIDE)], 0)
        far, at = (b3, j) if j < half else (b4, j - half)
        b = jnp.concatenate(
            [r[j * tg : (j + 1) * tg, :] for r in (b0, b1, b2)] + [far[at * tg : (at + 1) * tg, :]],
            0,
        )
        start = pl.multiple_of(row * BAND, 16)
        got_a = dot(pick_ref[row], a).astype(BF)
        got_b = dot(pick_ref[row], b).astype(BF)
        for e in range(2):
            out_ref[e, pl.ds(start, BAND), :width] = got_a[e * BAND : (e + 1) * BAND]
            out_ref[e, pl.ds(start, BAND), width:] = got_b[e * BAND : (e + 1) * BAND]


def pack_rows(pos, a_parts, b_parts, pick, blk, feats):
    tg = b_parts[0].shape[0] // SIDE
    specs = [pl.BlockSpec((p.shape[0], blk), lambda f, s: (0, f)) for p in a_parts + b_parts]
    return pl.pallas_call(
        functools.partial(pack_kernel, tg),
        out_shape=jax.ShapeDtypeStruct((2, ROWS, feats), BF),
        grid_spec=pltpu.PrefetchScalarGridSpec(
            num_scalar_prefetch=1,
            grid=(feats // (2 * blk),),
            in_specs=specs + [pl.BlockSpec(pick.shape, lambda f, s: (0, 0, 0))],
            out_specs=pl.BlockSpec((2, ROWS, 2 * blk), lambda f, s: (0, 0, f)),
        ),
        compiler_params=pltpu.CompilerParams(vmem_limit_bytes=56 * MIB),
        cost_estimate=pl.CostEstimate(
            flops=2 * 2 * ROWS * SIDE * tg * feats, transcendentals=0, bytes_accessed=14 * 2**20
        ),
        name="pack",
    )(pos, *a_parts, *b_parts, pick)


def pack_plain_kernel(rows_ref, pick_ref, out_ref):
    got = dot(pick_ref[0], rows_ref[...]).astype(BF)
    for e in range(2):
        out_ref[e] = got[e * BAND : (e + 1) * BAND]


def pack_plain(rows, pick, feats, blk=2048):
    depth = pick.shape[2]
    return pl.pallas_call(
        pack_plain_kernel,
        out_shape=jax.ShapeDtypeStruct((2, ROWS, feats), BF),
        grid=(SIDE, feats // blk),
        in_specs=[
            pl.BlockSpec((depth, blk), lambda y, f: (y, f)),
            pl.BlockSpec((1, 2 * BAND, depth), lambda y, f: (y, 0, 0)),
        ],
        out_specs=pl.BlockSpec((2, BAND, blk), lambda y, f: (0, y, f)),
        compiler_params=pltpu.CompilerParams(vmem_limit_bytes=56 * MIB),
        cost_estimate=pl.CostEstimate(flops=1, transcendentals=0, bytes_accessed=1),
        name="pack_plain",
    )(rows, pick)


def own_at(n):
    return lambda e, j, s: (e, 0, jnp.minimum(j, n - 1))


def other_at(n):
    return lambda e, j, s: (e, 0, jnp.maximum(j - n, 0))


def col_at(n):
    def at(e, j, s):
        first = j < n
        core = jnp.where(first, s[1], 1 - s[1])
        return (e, 0, core * n + jnp.where(first, j, j - n))

    return at


def pre_kernel(core_ref, own, other, wg, wu, out, x_buf, w_buf, sems):
    core = core_ref[0]
    hid = wg.shape[1]
    feats = own.shape[2]
    lo = pl.multiple_of(core * feats, feats)
    hi = pl.multiple_of((1 - core) * feats, feats)
    copies = []
    for e in range(2):
        copies += [
            pltpu.make_async_copy(own.at[e], x_buf.at[e, :, pl.ds(lo, feats)], sems.at[4 * e]),
            pltpu.make_async_copy(wg.at[e], w_buf.at[e, pl.ds(0, hid)], sems.at[4 * e + 1]),
            pltpu.make_async_copy(wu.at[e], w_buf.at[e, pl.ds(hid, hid)], sems.at[4 * e + 2]),
            pltpu.make_async_copy(other.at[e], x_buf.at[e, :, pl.ds(hi, feats)], sems.at[4 * e + 3]),
        ]
    for c in copies:
        c.start()
    for e in range(2):
        for c in copies[4 * e : 4 * e + 4]:
            c.wait()
        out[e] = dot_t(x_buf[e], w_buf[e])


ANY = pl.BlockSpec(memory_space=pl.ANY)
IN_VMEM = pl.BlockSpec(memory_space=pltpu.VMEM)
IN_SMEM = pl.BlockSpec(memory_space=pltpu.SMEM)


def pre_rows(core, own, other, w_gate, w_up):
    hid, width = w_gate.shape[1:]
    return pl.pallas_call(
        pre_kernel,
        out_shape=jax.ShapeDtypeStruct((2, ROWS, 2 * hid), F32),
        in_specs=[IN_SMEM, ANY, ANY, ANY, ANY],
        out_specs=IN_VMEM,
        scratch_shapes=[
            pltpu.VMEM((2, ROWS, width), BF),
            pltpu.VMEM((2, 2 * hid, width), BF),
            pltpu.SemaphoreType.DMA((8,)),
        ],
        compiler_params=pltpu.CompilerParams(vmem_limit_bytes=56 * MIB),
        cost_estimate=pl.CostEstimate(
            flops=2 * 4 * ROWS * hid * width, transcendentals=0, bytes_accessed=18 * 2**20
        ),
        name="pre",
    )(core, own, other, w_gate, w_up)


def mid_kernel(
    core_ref, own, other, wd, wg, wu, pre, g_ref,
    dx_a, keep_b, send_b, both_o, hid_o, score,
    y_buf, d_buf, w_buf, dx_buf, sems, out_sems,
):
    core = core_ref[0]
    hid, width = wd.shape[1:]
    feats = own.shape[2]
    part = width // 8
    lo = pl.multiple_of(core * feats, feats)
    hi = pl.multiple_of((1 - core) * feats, feats)
    order = (1, 0)
    copies = {}
    for e in order:
        copies[e] = [
            pltpu.make_async_copy(wd.at[e], d_buf.at[e], sems.at[5 * e]),
            pltpu.make_async_copy(own.at[e], y_buf.at[e, :, pl.ds(lo, feats)], sems.at[5 * e + 1]),
            pltpu.make_async_copy(other.at[e], y_buf.at[e, :, pl.ds(hi, feats)], sems.at[5 * e + 2]),
            pltpu.make_async_copy(wg.at[e], w_buf.at[e, pl.ds(0, hid)], sems.at[5 * e + 3]),
            pltpu.make_async_copy(wu.at[e], w_buf.at[e, pl.ds(hid, hid)], sems.at[5 * e + 4]),
        ]
    for c in copies[order[0]]:
        c.start()
    ends = []
    for e in order:
        gate, up, g = pre[e, :, :hid], pre[e, :, hid:], g_ref[e]
        s = jax.nn.sigmoid(gate)
        act = gate * s
        hidden = act * up
        slope = up * s * (1.0 + gate * (1.0 - s))
        hid_o[e] = (hidden * g).astype(BF)
        for c in copies[e][:3]:
            c.wait()
        if e == order[0]:
            for c in copies[order[1]]:
                c.start()
        dy = dot_t(y_buf[e], d_buf[e])
        score[e] = jnp.sum(hidden * dy, axis=1, keepdims=True)
        d_hid = dy * g
        both = jnp.concatenate([d_hid * slope, d_hid * act], 1)
        both_o[e] = both.astype(BF)
        for c in copies[e][3:]:
            c.wait()
        if e == 0:
            left = both.astype(BF)
            for k in range(4):
                cols = pl.ds(k * 2 * part, 2 * part)
                dx_buf[e, pl.ds(0, ROWS), cols] = dot(left, w_buf[e, :, cols]).astype(BF)
                c = pltpu.make_async_copy(
                    dx_buf.at[e, pl.ds(0, ROWS), cols], dx_a.at[:, cols], out_sems.at[8 + k]
                )
                c.start()
                ends.append(c)
        else:
            gap = jnp.zeros((PAD - CAP, 2 * hid), F32)
            rows = []
            for i in range(SIDE * SIDE):
                rows += [both[i * CAP : (i + 1) * CAP], gap]
            left = jnp.concatenate(rows, 0).astype(BF)
            for k in range(8):
                cols = pl.ds(k * part, part)
                to = pl.ds(k // 2 * part, part)
                dx_buf[e, :, cols] = dot(left, w_buf[e, :, cols]).astype(BF)
                kept = pltpu.make_async_copy(dx_buf.at[e, :, cols], keep_b.at[:, to], out_sems.at[k])
                sent = pltpu.make_async_copy(dx_buf.at[e, :, cols], send_b.at[:, to], out_sems.at[k])

                @pl.when(core == k % 2)
                def _():
                    kept.start()

                @pl.when(core != k % 2)
                def _():
                    sent.start()

                ends.append(kept)
    for c in ends:
        c.wait()


def mid_rows(core, own, other, w_down, w_gate, w_up, pre, g):
    hid, width = w_down.shape[1:]
    tall = SIDE * SIDE * PAD
    return pl.pallas_call(
        mid_kernel,
        out_shape=[
            jax.ShapeDtypeStruct((ROWS, width), BF),
            jax.ShapeDtypeStruct((tall, width // 2), BF),
            jax.ShapeDtypeStruct((tall, width // 2), BF),
            jax.ShapeDtypeStruct((2, ROWS, 2 * hid), BF),
            jax.ShapeDtypeStruct((2, ROWS, hid), BF),
            jax.ShapeDtypeStruct((2, ROWS, 1), F32),
        ],
        in_specs=[IN_SMEM, ANY, ANY, ANY, ANY, ANY, IN_VMEM, IN_VMEM],
        out_specs=[ANY, ANY, ANY, IN_VMEM, IN_VMEM, IN_VMEM],
        scratch_shapes=[
            pltpu.VMEM((2, ROWS, width), BF),
            pltpu.VMEM((2, hid, width), BF),
            pltpu.VMEM((2, 2 * hid, width), BF),
            pltpu.VMEM((2, tall, width), BF),
            pltpu.SemaphoreType.DMA((10,)),
            pltpu.SemaphoreType.DMA((12,)),
        ],
        compiler_params=pltpu.CompilerParams(vmem_limit_bytes=56 * MIB),
        cost_estimate=pl.CostEstimate(
            flops=2 * 6 * ROWS * hid * width,
            transcendentals=2 * ROWS * hid,
            bytes_accessed=34 * 2**20,
        ),
        name="mid",
    )(core, own, other, w_down, w_gate, w_up, pre, g)


def grad_kernel(n, pos_ref, x_own, x_other, y_own, y_other, both_o, hid_o, gg, gu, gd):
    j = pl.program_id(1)
    hid = gg.shape[1]

    def put(x, y):
        r = t_dot(both_o[0], x)
        gg[0] = r[:hid].astype(BF)
        gu[0] = r[hid:].astype(BF)
        gd[0] = t_dot(hid_o[0], y).astype(BF)

    @pl.when(j < n)
    def _():
        put(x_own[0], y_own[0])

    @pl.when(j >= n)
    def _():
        put(x_other[0], y_other[0])


def grad_rows(pos, x_own, x_other, y_own, y_other, both_o, hid_o, blk=1024):
    hid = hid_o.shape[2]
    n = x_own.shape[2] // blk
    whole = lambda e, j, s: (e, 0, 0)
    return pl.pallas_call(
        functools.partial(grad_kernel, n),
        out_shape=[jax.ShapeDtypeStruct((2, hid, 2 * n * blk), BF)] * 3,
        grid_spec=pltpu.PrefetchScalarGridSpec(
            num_scalar_prefetch=1,
            grid=(2, 2 * n),
            in_specs=[
                pl.BlockSpec((1, ROWS, blk), own_at(n)),
                pl.BlockSpec((1, ROWS, blk), other_at(n)),
                pl.BlockSpec((1, ROWS, blk), own_at(n)),
                pl.BlockSpec((1, ROWS, blk), other_at(n)),
                pl.BlockSpec((1, ROWS, 2 * hid), whole),
                pl.BlockSpec((1, ROWS, hid), whole),
            ],
            out_specs=[pl.BlockSpec((1, hid, blk), col_at(n))] * 3,
        ),
        compiler_params=pltpu.CompilerParams(vmem_limit_bytes=56 * MIB),
        cost_estimate=pl.CostEstimate(
            flops=2 * 6 * ROWS * hid * n * 2 * blk, transcendentals=0, bytes_accessed=30 * 2**20
        ),
        name="grads",
    )(pos, x_own, x_other, y_own, y_other, both_o, hid_o)


def before_count(member):
    t = member.shape[-1]
    upper = (jnp.arange(t)[:, None] < jnp.arange(t)[None, :]).astype(BF)
    return jnp.dot(member.astype(BF), upper, preferred_element_type=F32).astype(jnp.int32)


def on_device(tokens, cotangent, gate_values, expert_ids, w_gate, w_up, w_down):
    tg, top = expert_ids.shape
    width = tokens.shape[1]
    n_exp = lax.axis_size("expert")
    experts = 2 * n_exp
    me = lax.axis_index("expert")
    lane = lax.axis_index("tensor")
    y, z, core = me // SIDE, me % SIDE, lane % 2
    pos = jnp.stack([y, core]).astype(jnp.int32)
    feats = width // 2
    blk = 512

    def half(v):
        return lax.dynamic_slice_in_dim(v, core * feats, feats, 1)

    x_all = lax.all_gather(half(tokens), "expert", axis=0, tiled=True)
    y_half = half(cotangent).reshape(tg, feats // (2 * blk), 2, blk)
    ya = y_half[:, :, 0].reshape(tg, feats // 2)
    yb = y_half[:, :, 1].reshape(tg, feats // 2)
    ya1 = jnp.concatenate(ring(ya, "z"), 0)
    yb1 = jnp.concatenate(ring(yb, "y"), 0)
    ya_parts, yb_parts = near(ya1, "y"), near(yb1, "z")

    route = jnp.concatenate([expert_ids.astype(BF), gate_values], 1)
    route = route.reshape(2 * tg * top // 128, 128)
    route = after_all(jnp.tile(route, (n_exp, 1)), (ya_parts, yb_parts))
    route = lax.all_to_all(route, "expert", split_axis=0, concat_axis=0, tiled=True)
    tab = route.reshape(SIDE, SIDE, tg, 2 * top)
    ids = tab[..., :top].astype(jnp.int32)
    gates = tab[..., top:].astype(F32)
    mine = 2 * me + jnp.arange(2)
    named = ids[None] == mine[:, None, None, None, None]
    member = jnp.any(named, -1)
    weight = jnp.sum(jnp.where(named, gates[None], 0.0), -1)
    count = before_count(member)
    target = jnp.where(member, jnp.arange(SIDE)[None, None, :, None] * CAP + count, -1)

    def hits(v):
        return v.reshape(2, SIDE, 1, SIDE * tg) == jnp.arange(BAND)[None, None, :, None]

    def picks(v):
        return hits(v).astype(BF).transpose(1, 0, 2, 3).reshape(SIDE, 2 * BAND, SIDE * tg)

    pick = picks(target)
    pick_ring = picks(target[:, :, (z + jnp.array(OFFS)) % SIDE])
    g_slot = jnp.sum(jnp.where(hits(target), weight.reshape(2, SIDE, 1, SIDE * tg), 0.0), -1)
    g_slot = g_slot.reshape(2, ROWS, 1)

    ya_parts, yb_parts = ya_parts + far(ya_parts, "y"), yb_parts + far(yb_parts, "z")
    x_own = pack_plain(x_all, pick, feats)
    x_other = swap_core(x_own)
    ya_parts, yb_parts = after_all((ya_parts, yb_parts), x_own)
    y_own = pack_rows(pos, ya_parts, yb_parts, pick_ring, blk, feats)
    pre = pre_rows(core.astype(jnp.int32).reshape(1), x_own, x_other, w_gate, w_up)
    cores = core.astype(jnp.int32).reshape(1)
    y_other = swap_core(y_own)
    dx_a, keep_b, send_b, both_o, hid_o, score = mid_rows(
        cores, y_own, y_other, w_down, w_gate, w_up, pre, g_slot
    )

    n_ten = lax.axis_size("tensor")
    part = width // n_ten
    share = lax.psum_scatter(dx_a, "tensor", scatter_dimension=1, tiled=True)
    came = swap_core(send_b)
    out_b = (keep_b.astype(F32) + came.astype(F32)).astype(BF)
    back_b = lax.all_to_all(out_b, "expert", split_axis=0, concat_axis=0, tiled=True)
    both_o, hid_o = after_all((both_o, hid_o), out_b)
    grads = grad_rows(pos, x_own, x_other, y_own, y_other, both_o, hid_o)

    total = score.reshape(ROWS * 2 // 128, 128)
    for bit in (1, 2, 4):
        total = total + lax.ppermute(total, "tensor", [(i, i ^ bit) for i in range(n_ten)])

    own_named = expert_ids[:, :, None] == jnp.arange(experts)[None, None, :]
    own_member = jnp.any(own_named, 1)
    own_count = before_count(own_member.T).T
    own_hit = own_member[:, :, None] & (own_count[:, :, None] == jnp.arange(PAD)[None, None, :])
    spread = own_hit.astype(BF).reshape(tg, n_exp, 2, PAD)
    spread_a, spread_b = spread[:, :, 0], spread[:, :, 1]

    back = jnp.pad(share.reshape(n_exp, CAP, part), ((0, 0), (0, PAD - CAP), (0, 0)))
    line = total.reshape(2, n_exp, CAP).transpose(1, 0, 2).reshape(n_exp, 1, 2 * CAP).astype(BF)
    line = jnp.pad(line, ((0, 0), (0, 7), (0, part - 2 * CAP)))
    back = jnp.concatenate([back, line], 1)
    back, grads = lax.optimization_barrier((back, grads))
    back = lax.all_to_all(back, "expert", split_axis=0, concat_axis=0, tiled=True)
    sum_b = jnp.einsum(
        "tns,nsf->tf",
        spread_b,
        back_b.reshape(n_exp, PAD, width // 2),
        preferred_element_type=F32,
    ).astype(BF)
    x = lane // 2
    mine_b = lax.dynamic_slice_in_dim(sum_b, x * part, part, 1).astype(F32)
    for step in range(1, n_ten // 2):
        piece = lax.dynamic_slice_in_dim(sum_b, (x + step) % (n_ten // 2) * part, part, 1)
        perm = [(i, (i + 2 * step) % n_ten) for i in range(n_ten)]
        mine_b = mine_b + lax.ppermute(piece, "tensor", perm).astype(F32)

    sum_a = jnp.einsum("tns,nsf->tf", spread_a, back[:, :PAD], preferred_element_type=F32)
    d_tokens = (sum_a + mine_b).astype(BF)
    scores = back[:, PAD, : 2 * CAP].reshape(experts, CAP).astype(F32)
    by_expert = jnp.sum(jnp.where(own_hit[:, :, :CAP], scores[None], 0.0), 2)
    d_gates = jnp.sum(jnp.where(own_named, by_expert[:, None, :], 0.0), 2).astype(BF)
    return (d_tokens, d_gates) + tuple(grads)


def solution(mesh):
    placed = (
        P("expert", None),
        P("expert", None),
        P("expert", None),
        P("expert", None),
        P("expert", "tensor", None),
        P("expert", "tensor", None),
        P("expert", "tensor", None),
    )
    return jax.shard_map(
        on_device,
        mesh=mesh,
        in_specs=placed,
        out_specs=(
            P("expert", "tensor"),
            P("expert", None),
            P("expert", "tensor", None),
            P("expert", "tensor", None),
            P("expert", "tensor", None),
        ),
        check_vma=False,
    )
```

```python
import functools

import jax
import jax.numpy as jnp
from jax import lax
from jax.experimental import pallas as pl
from jax.experimental.pallas import tpu as pltpu
from jax.sharding import PartitionSpec as P

BF = jnp.bfloat16
F32 = jnp.float32
SIDE = 4
OFFS = (0, 3, 1, 2)
CAP = 36
ROWS = SIDE * SIDE * CAP
BAND = SIDE * CAP
PAD = 40
MIB = 1024 * 1024


def dot(a, b):
    return lax.dot_general(a, b, (((1,), (0,)), ((), ())), preferred_element_type=F32)


def dot_t(a, b):
    return lax.dot_general(a, b, (((1,), (1,)), ((), ())), preferred_element_type=F32)


def t_dot(a, b):
    return lax.dot_general(a, b, (((0,), (0,)), ((), ())), preferred_element_type=F32)


def shift(v, axis, step):
    perm = []
    for y in range(SIDE):
        for z in range(SIDE):
            to = ((y + step) % SIDE, z) if axis == "y" else (y, (z + step) % SIDE)
            perm.append((y * SIDE + z, to[0] * SIDE + to[1]))
    return lax.ppermute(v, "expert", perm)


def swap_core(v):
    n = lax.axis_size("tensor")
    return lax.ppermute(v, "tensor", [(i, i ^ 1) for i in range(n)])


def near(v, axis):
    return (v, shift(v, axis, 1), shift(v, axis, -1))


def far(blocks, axis, half=None):
    v, before, after = blocks
    half = half or v.shape[0] // 2
    return (shift(before[:half], axis, 1), shift(after[half:], axis, -1))


def ring(v, axis, half=None):
    blocks = near(v, axis)
    return blocks + far(blocks, axis, half)


def after_all(values, others):
    return lax.optimization_barrier((values, others))[0]


def pack_kernel(tg, pos_ref, a0, a1, a2, a3, a4, b0, b1, b2, b3, b4, pick_ref, out_ref):
    y = pos_ref[0]
    width = a0.shape[1]
    a_parts = (a0, a1, a2, (a3, a4))
    half = SIDE // 2
    for j, off in enumerate(OFFS):
        row = lax.rem(y + off, SIDE)
        if j < 3:
            a = a_parts[j][...]
        else:
            a = jnp.concatenate([a3[...], a4[...]], 0)
        step = a.shape[0] // SIDE
        a = jnp.concatenate([a[i * step : i * step + tg] for i in range(SIDE)], 0)
        far, at = (b3, j) if j < half else (b4, j - half)
        b = jnp.concatenate(
            [r[j * tg : (j + 1) * tg, :] for r in (b0, b1, b2)] + [far[at * tg : (at + 1) * tg, :]],
            0,
        )
        start = pl.multiple_of(row * BAND, 16)
        got_a = dot(pick_ref[row], a).astype(BF)
        got_b = dot(pick_ref[row], b).astype(BF)
        for e in range(2):
            out_ref[e, pl.ds(start, BAND), :width] = got_a[e * BAND : (e + 1) * BAND]
            out_ref[e, pl.ds(start, BAND), width:] = got_b[e * BAND : (e + 1) * BAND]


def pack_rows(pos, a_parts, b_parts, pick, blk, feats):
    tg = b_parts[0].shape[0] // SIDE
    specs = [pl.BlockSpec((p.shape[0], blk), lambda f, s: (0, f)) for p in a_parts + b_parts]
    return pl.pallas_call(
        functools.partial(pack_kernel, tg),
        out_shape=jax.ShapeDtypeStruct((2, ROWS, feats), BF),
        grid_spec=pltpu.PrefetchScalarGridSpec(
            num_scalar_prefetch=1,
            grid=(feats // (2 * blk),),
            in_specs=specs + [pl.BlockSpec(pick.shape, lambda f, s: (0, 0, 0))],
            out_specs=pl.BlockSpec((2, ROWS, 2 * blk), lambda f, s: (0, 0, f)),
        ),
        compiler_params=pltpu.CompilerParams(vmem_limit_bytes=56 * MIB),
        cost_estimate=pl.CostEstimate(
            flops=2 * 2 * ROWS * SIDE * tg * feats, transcendentals=0, bytes_accessed=14 * 2**20
        ),
        name="pack",
    )(pos, *a_parts, *b_parts, pick)


def pack_plain_kernel(rows_ref, pick_ref, out_ref):
    got = dot(pick_ref[0], rows_ref[...]).astype(BF)
    for e in range(2):
        out_ref[e] = got[e * BAND : (e + 1) * BAND]


def pack_plain(rows, pick, feats, blk=2048):
    depth = pick.shape[2]
    return pl.pallas_call(
        pack_plain_kernel,
        out_shape=jax.ShapeDtypeStruct((2, ROWS, feats), BF),
        grid=(SIDE, feats // blk),
        in_specs=[
            pl.BlockSpec((depth, blk), lambda y, f: (y, f)),
            pl.BlockSpec((1, 2 * BAND, depth), lambda y, f: (y, 0, 0)),
        ],
        out_specs=pl.BlockSpec((2, BAND, blk), lambda y, f: (0, y, f)),
        compiler_params=pltpu.CompilerParams(vmem_limit_bytes=56 * MIB),
        cost_estimate=pl.CostEstimate(flops=1, transcendentals=0, bytes_accessed=1),
        name="pack_plain",
    )(rows, pick)


def own_at(n):
    return lambda e, j, s: (e, 0, jnp.minimum(j, n - 1))


def other_at(n):
    return lambda e, j, s: (e, 0, jnp.maximum(j - n, 0))


def col_at(n):
    def at(e, j, s):
        first = j < n
        core = jnp.where(first, s[1], 1 - s[1])
        return (e, 0, core * n + jnp.where(first, j, j - n))

    return at


def pre_kernel(core_ref, own, other, wg, wu, out, x_buf, w_buf, sems):
    core = core_ref[0]
    hid = wg.shape[1]
    feats = own.shape[2]
    lo = pl.multiple_of(core * feats, feats)
    hi = pl.multiple_of((1 - core) * feats, feats)
    copies = []
    for e in range(2):
        copies += [
            pltpu.make_async_copy(own.at[e], x_buf.at[e, :, pl.ds(lo, feats)], sems.at[4 * e]),
            pltpu.make_async_copy(wg.at[e], w_buf.at[e, pl.ds(0, hid)], sems.at[4 * e + 1]),
            pltpu.make_async_copy(wu.at[e], w_buf.at[e, pl.ds(hid, hid)], sems.at[4 * e + 2]),
            pltpu.make_async_copy(other.at[e], x_buf.at[e, :, pl.ds(hi, feats)], sems.at[4 * e + 3]),
        ]
    for c in copies:
        c.start()
    for e in range(2):
        for c in copies[4 * e : 4 * e + 4]:
            c.wait()
        out[e] = dot_t(x_buf[e], w_buf[e])


ANY = pl.BlockSpec(memory_space=pl.ANY)
IN_VMEM = pl.BlockSpec(memory_space=pltpu.VMEM)
IN_SMEM = pl.BlockSpec(memory_space=pltpu.SMEM)


def pre_rows(core, own, other, w_gate, w_up):
    hid, width = w_gate.shape[1:]
    return pl.pallas_call(
        pre_kernel,
        out_shape=jax.ShapeDtypeStruct((2, ROWS, 2 * hid), F32),
        in_specs=[IN_SMEM, ANY, ANY, ANY, ANY],
        out_specs=IN_VMEM,
        scratch_shapes=[
            pltpu.VMEM((2, ROWS, width), BF),
            pltpu.VMEM((2, 2 * hid, width), BF),
            pltpu.SemaphoreType.DMA((8,)),
        ],
        compiler_params=pltpu.CompilerParams(vmem_limit_bytes=56 * MIB),
        cost_estimate=pl.CostEstimate(
            flops=2 * 4 * ROWS * hid * width, transcendentals=0, bytes_accessed=18 * 2**20
        ),
        name="pre",
    )(core, own, other, w_gate, w_up)


def mid_kernel(
    core_ref, own, other, wd, wg, wu, pre, g_ref,
    dx_a, keep_b, send_b, both_o, hid_o, score,
    y_buf, d_buf, w_buf, dx_buf, few_buf, sems, out_sems,
):
    core = core_ref[0]
    hid, width = wd.shape[1:]
    feats = own.shape[2]
    part = width // 8
    few = part // 4
    lo = pl.multiple_of(core * feats, feats)
    hi = pl.multiple_of((1 - core) * feats, feats)
    order = (1, 0)
    copies = {}
    for e in order:
        copies[e] = [
            pltpu.make_async_copy(wd.at[e], d_buf.at[e], sems.at[5 * e]),
            pltpu.make_async_copy(own.at[e], y_buf.at[e, :, pl.ds(lo, feats)], sems.at[5 * e + 1]),
            pltpu.make_async_copy(other.at[e], y_buf.at[e, :, pl.ds(hi, feats)], sems.at[5 * e + 2]),
            pltpu.make_async_copy(wg.at[e], w_buf.at[e, pl.ds(0, hid)], sems.at[5 * e + 3]),
            pltpu.make_async_copy(wu.at[e], w_buf.at[e, pl.ds(hid, hid)], sems.at[5 * e + 4]),
        ]
    for c in copies[order[0]]:
        c.start()
    ends = []
    for e in order:
        gate, up, g = pre[e, :, :hid], pre[e, :, hid:], g_ref[e]
        s = jax.nn.sigmoid(gate)
        act = gate * s
        hidden = act * up
        slope = up * s * (1.0 + gate * (1.0 - s))
        hid_o[e] = (hidden * g).astype(BF)
        for c in copies[e][:3]:
            c.wait()
        if e == order[0]:
            for c in copies[order[1]]:
                c.start()
        dy = dot_t(y_buf[e], d_buf[e])
        score[e] = jnp.sum(hidden * dy, axis=1, keepdims=True)
        d_hid = dy * g
        both = jnp.concatenate([d_hid * slope, d_hid * act], 1)
        both_o[e] = both.astype(BF)
        for c in copies[e][3:]:
            c.wait()
        if e == 0:
            left = both.astype(BF)
            for k in range(8):
                cols = pl.ds(k * part, part)
                dx_buf[e, pl.ds(0, ROWS), cols] = dot(left, w_buf[e, :, cols]).astype(BF)
                c = pltpu.make_async_copy(
                    dx_buf.at[e, pl.ds(0, ROWS), cols],
                    dx_a.at[k, :, pl.ds(0, part)],
                    out_sems.at[8 + k],
                )
                c.start()
                ends.append(c)
        else:
            gap = jnp.zeros((PAD - CAP, 2 * hid), F32)
            rows = []
            for i in range(SIDE * SIDE):
                rows += [both[i * CAP : (i + 1) * CAP], gap]
            left = jnp.concatenate(rows, 0).astype(BF)
            for k in range(8):
                cols = pl.ds(k * part + few, part - few)
                to = pl.ds(k // 2 * (part - few), part - few)
                dx_buf[e, :, cols] = dot(left, w_buf[e, :, cols]).astype(BF)
                kept = pltpu.make_async_copy(dx_buf.at[e, :, cols], keep_b.at[:, to], out_sems.at[k])
                sent = pltpu.make_async_copy(dx_buf.at[e, :, cols], send_b.at[:, to], out_sems.at[k])

                @pl.when(core == k % 2)
                def _():
                    kept.start()

                @pl.when(core != k % 2)
                def _():
                    sent.start()

                ends.append(kept)
            left = both.astype(BF)
            for k in range(8):
                at = pl.ds(k * few, few)
                few_buf[:, at] = dot(left, w_buf[e, :, pl.ds(k * part, few)]).astype(BF)
                c = pltpu.make_async_copy(
                    few_buf.at[:, at],
                    dx_a.at[k, :, pl.ds(part, few)],
                    out_sems.at[16 + k],
                )
                c.start()
                ends.append(c)
    for c in ends:
        c.wait()


def mid_rows(core, own, other, w_down, w_gate, w_up, pre, g):
    hid, width = w_down.shape[1:]
    tall = SIDE * SIDE * PAD
    return pl.pallas_call(
        mid_kernel,
        out_shape=[
            jax.ShapeDtypeStruct((8, ROWS, width // 8 + width // 32), BF),
            jax.ShapeDtypeStruct((tall, width * 3 // 8), BF),
            jax.ShapeDtypeStruct((tall, width * 3 // 8), BF),
            jax.ShapeDtypeStruct((2, ROWS, 2 * hid), BF),
            jax.ShapeDtypeStruct((2, ROWS, hid), BF),
            jax.ShapeDtypeStruct((2, ROWS, 1), F32),
        ],
        in_specs=[IN_SMEM, ANY, ANY, ANY, ANY, ANY, IN_VMEM, IN_VMEM],
        out_specs=[ANY, ANY, ANY, IN_VMEM, IN_VMEM, IN_VMEM],
        scratch_shapes=[
            pltpu.VMEM((2, ROWS, width), BF),
            pltpu.VMEM((2, hid, width), BF),
            pltpu.VMEM((2, 2 * hid, width), BF),
            pltpu.VMEM((2, tall, width), BF),
            pltpu.VMEM((ROWS, width // 4), BF),
            pltpu.SemaphoreType.DMA((10,)),
            pltpu.SemaphoreType.DMA((24,)),
        ],
        compiler_params=pltpu.CompilerParams(vmem_limit_bytes=56 * MIB),
        cost_estimate=pl.CostEstimate(
            flops=2 * 6 * ROWS * hid * width,
            transcendentals=2 * ROWS * hid,
            bytes_accessed=34 * 2**20,
        ),
        name="mid",
    )(core, own, other, w_down, w_gate, w_up, pre, g)


def grad_kernel(n, pos_ref, x_own, x_other, y_own, y_other, both_o, hid_o, gg, gu, gd):
    j = pl.program_id(1)
    hid = gg.shape[1]

    def put(x, y):
        r = t_dot(both_o[0], x)
        gg[0] = r[:hid].astype(BF)
        gu[0] = r[hid:].astype(BF)
        gd[0] = t_dot(hid_o[0], y).astype(BF)

    @pl.when(j < n)
    def _():
        put(x_own[0], y_own[0])

    @pl.when(j >= n)
    def _():
        put(x_other[0], y_other[0])


def grad_rows(pos, x_own, x_other, y_own, y_other, both_o, hid_o, blk=1024):
    hid = hid_o.shape[2]
    n = x_own.shape[2] // blk
    whole = lambda e, j, s: (e, 0, 0)
    return pl.pallas_call(
        functools.partial(grad_kernel, n),
        out_shape=[jax.ShapeDtypeStruct((2, hid, 2 * n * blk), BF)] * 3,
        grid_spec=pltpu.PrefetchScalarGridSpec(
            num_scalar_prefetch=1,
            grid=(2, 2 * n),
            in_specs=[
                pl.BlockSpec((1, ROWS, blk), own_at(n)),
                pl.BlockSpec((1, ROWS, blk), other_at(n)),
                pl.BlockSpec((1, ROWS, blk), own_at(n)),
                pl.BlockSpec((1, ROWS, blk), other_at(n)),
                pl.BlockSpec((1, ROWS, 2 * hid), whole),
                pl.BlockSpec((1, ROWS, hid), whole),
            ],
            out_specs=[pl.BlockSpec((1, hid, blk), col_at(n))] * 3,
        ),
        compiler_params=pltpu.CompilerParams(vmem_limit_bytes=56 * MIB),
        cost_estimate=pl.CostEstimate(
            flops=2 * 6 * ROWS * hid * n * 2 * blk, transcendentals=0, bytes_accessed=30 * 2**20
        ),
        name="grads",
    )(pos, x_own, x_other, y_own, y_other, both_o, hid_o)


def before_count(member):
    t = member.shape[-1]
    upper = (jnp.arange(t)[:, None] < jnp.arange(t)[None, :]).astype(BF)
    return jnp.dot(member.astype(BF), upper, preferred_element_type=F32).astype(jnp.int32)


def on_device(tokens, cotangent, gate_values, expert_ids, w_gate, w_up, w_down):
    tg, top = expert_ids.shape
    width = tokens.shape[1]
    n_exp = lax.axis_size("expert")
    experts = 2 * n_exp
    me = lax.axis_index("expert")
    lane = lax.axis_index("tensor")
    y, z, core = me // SIDE, me % SIDE, lane % 2
    pos = jnp.stack([y, core]).astype(jnp.int32)
    feats = width // 2
    blk = 512

    def half(v):
        return lax.dynamic_slice_in_dim(v, core * feats, feats, 1)

    x_all = lax.all_gather(half(tokens), "expert", axis=0, tiled=True)
    y_half = half(cotangent).reshape(tg, feats // (2 * blk), 2, blk)
    ya = y_half[:, :, 0].reshape(tg, feats // 2)
    yb = y_half[:, :, 1].reshape(tg, feats // 2)
    ya1 = jnp.concatenate(ring(ya, "z"), 0)
    yb1 = jnp.concatenate(ring(yb, "y"), 0)
    ya_parts, yb_parts = near(ya1, "y"), near(yb1, "z")

    route = jnp.concatenate([expert_ids.astype(BF), gate_values], 1)
    route = route.reshape(2 * tg * top // 128, 128)
    route = after_all(jnp.tile(route, (n_exp, 1)), (ya_parts, yb_parts))
    route = lax.all_to_all(route, "expert", split_axis=0, concat_axis=0, tiled=True)
    tab = route.reshape(SIDE, SIDE, tg, 2 * top)
    ids = tab[..., :top].astype(jnp.int32)
    gates = tab[..., top:].astype(F32)
    mine = 2 * me + jnp.arange(2)
    named = ids[None] == mine[:, None, None, None, None]
    member = jnp.any(named, -1)
    weight = jnp.sum(jnp.where(named, gates[None], 0.0), -1)
    count = before_count(member)
    target = jnp.where(member, jnp.arange(SIDE)[None, None, :, None] * CAP + count, -1)

    def hits(v):
        return v.reshape(2, SIDE, 1, SIDE * tg) == jnp.arange(BAND)[None, None, :, None]

    def picks(v):
        return hits(v).astype(BF).transpose(1, 0, 2, 3).reshape(SIDE, 2 * BAND, SIDE * tg)

    pick = picks(target)
    pick_ring = picks(target[:, :, (z + jnp.array(OFFS)) % SIDE])
    g_slot = jnp.sum(jnp.where(hits(target), weight.reshape(2, SIDE, 1, SIDE * tg), 0.0), -1)
    g_slot = g_slot.reshape(2, ROWS, 1)

    ya_parts, yb_parts = ya_parts + far(ya_parts, "y"), yb_parts + far(yb_parts, "z")
    x_own = pack_plain(x_all, pick, feats)
    x_other = swap_core(x_own)
    ya_parts, yb_parts = after_all((ya_parts, yb_parts), x_own)
    y_own = pack_rows(pos, ya_parts, yb_parts, pick_ring, blk, feats)
    pre = pre_rows(core.astype(jnp.int32).reshape(1), x_own, x_other, w_gate, w_up)
    cores = core.astype(jnp.int32).reshape(1)
    y_other = swap_core(y_own)
    dx_a, keep_b, send_b, both_o, hid_o, score = mid_rows(
        cores, y_own, y_other, w_down, w_gate, w_up, pre, g_slot
    )

    n_ten = lax.axis_size("tensor")
    part = width // n_ten
    few = part // 4
    rest = part - few
    share = lax.psum_scatter(dx_a, "tensor", scatter_dimension=0, tiled=True)
    came = swap_core(send_b)
    out_b = (keep_b.astype(F32) + came.astype(F32)).astype(BF)
    back_b = lax.all_to_all(out_b, "expert", split_axis=0, concat_axis=0, tiled=True)
    both_o, hid_o = after_all((both_o, hid_o), out_b)
    grads = grad_rows(pos, x_own, x_other, y_own, y_other, both_o, hid_o)

    total = score.reshape(ROWS * 2 // 128, 128)
    for bit in (1, 2, 4):
        total = total + lax.ppermute(total, "tensor", [(i, i ^ bit) for i in range(n_ten)])

    own_named = expert_ids[:, :, None] == jnp.arange(experts)[None, None, :]
    own_member = jnp.any(own_named, 1)
    own_count = before_count(own_member.T).T
    own_hit = own_member[:, :, None] & (own_count[:, :, None] == jnp.arange(PAD)[None, None, :])
    spread = own_hit.astype(BF).reshape(tg, n_exp, 2, PAD)
    spread_a, spread_b = spread[:, :, 0], spread[:, :, 1]

    line = total.reshape(2, n_exp, CAP).transpose(1, 0, 2).reshape(n_exp, 1, 2 * CAP).astype(BF)
    line = jnp.pad(line, ((0, 0), (0, PAD - CAP - 1), (0, part + few - 2 * CAP)))
    back = jnp.concatenate([share.reshape(n_exp, CAP, part + few), line], 1)
    back, grads = lax.optimization_barrier((back, grads))
    back = lax.all_to_all(back, "expert", split_axis=0, concat_axis=0, tiled=True)
    sum_b = jnp.einsum(
        "tns,nsf->tf",
        spread_b,
        back_b.reshape(n_exp, PAD, width * 3 // 8),
        preferred_element_type=F32,
    ).astype(BF)
    x = lane // 2
    mine_b = lax.dynamic_slice_in_dim(sum_b, x * rest, rest, 1).astype(F32)
    for step in range(1, n_ten // 2):
        piece = lax.dynamic_slice_in_dim(sum_b, (x + step) % (n_ten // 2) * rest, rest, 1)
        perm = [(i, (i + 2 * step) % n_ten) for i in range(n_ten)]
        mine_b = mine_b + lax.ppermute(piece, "tensor", perm).astype(F32)

    sum_a = jnp.einsum("tns,nsf->tf", spread_a, back[:, :, :part], preferred_element_type=F32)
    sum_few = jnp.einsum("tns,nsf->tf", spread_b, back[:, :, part:], preferred_element_type=F32)
    d_tokens = (sum_a + jnp.concatenate([sum_few, mine_b], 1)).astype(BF)
    scores = back[:, CAP, : 2 * CAP].reshape(experts, CAP).astype(F32)
    by_expert = jnp.sum(jnp.where(own_hit[:, :, :CAP], scores[None], 0.0), 2)
    d_gates = jnp.sum(jnp.where(own_named, by_expert[:, None, :], 0.0), 2).astype(BF)
    return (d_tokens, d_gates) + tuple(grads)


def solution(mesh):
    placed = (
        P("expert", None),
        P("expert", None),
        P("expert", None),
        P("expert", None),
        P("expert", "tensor", None),
        P("expert", "tensor", None),
        P("expert", "tensor", None),
    )
    return jax.shard_map(
        on_device,
        mesh=mesh,
        in_specs=placed,
        out_specs=(
            P("expert", "tensor"),
            P("expert", None),
            P("expert", "tensor", None),
            P("expert", "tensor", None),
            P("expert", "tensor", None),
        ),
        check_vma=False,
    )
```

```python
import functools

import jax
import jax.numpy as jnp
from jax import lax
from jax.experimental import pallas as pl
from jax.experimental.pallas import tpu as pltpu
from jax.sharding import PartitionSpec as P

BF = jnp.bfloat16
F32 = jnp.float32
SIDE = 4
OFFS = (0, 3, 1, 2)
CAP = 36
ROWS = SIDE * SIDE * CAP
BAND = SIDE * CAP
PAD = 40
MIB = 1024 * 1024


def dot(a, b):
    return lax.dot_general(a, b, (((1,), (0,)), ((), ())), preferred_element_type=F32)


def dot_t(a, b):
    return lax.dot_general(a, b, (((1,), (1,)), ((), ())), preferred_element_type=F32)


def t_dot(a, b):
    return lax.dot_general(a, b, (((0,), (0,)), ((), ())), preferred_element_type=F32)


def shift(v, axis, step):
    perm = []
    for y in range(SIDE):
        for z in range(SIDE):
            to = ((y + step) % SIDE, z) if axis == "y" else (y, (z + step) % SIDE)
            perm.append((y * SIDE + z, to[0] * SIDE + to[1]))
    return lax.ppermute(v, "expert", perm)


def swap_core(v):
    n = lax.axis_size("tensor")
    return lax.ppermute(v, "tensor", [(i, i ^ 1) for i in range(n)])


def near(v, axis):
    return (v, shift(v, axis, 1), shift(v, axis, -1))


def far(blocks, axis, half=None):
    v, before, after = blocks
    half = half or v.shape[0] // 2
    return (shift(before[:half], axis, 1), shift(after[half:], axis, -1))


def ring(v, axis, half=None):
    blocks = near(v, axis)
    return blocks + far(blocks, axis, half)


def after_all(values, others):
    return lax.optimization_barrier((values, others))[0]


def pack_kernel(tg, pos_ref, a0, a1, a2, a3, a4, b0, b1, b2, b3, b4, pick_ref, out_ref):
    y = pos_ref[0]
    width = a0.shape[1]
    a_parts = (a0, a1, a2, (a3, a4))
    half = SIDE // 2
    for j, off in enumerate(OFFS):
        row = lax.rem(y + off, SIDE)
        if j < 3:
            a = a_parts[j][...]
        else:
            a = jnp.concatenate([a3[...], a4[...]], 0)
        step = a.shape[0] // SIDE
        a = jnp.concatenate([a[i * step : i * step + tg] for i in range(SIDE)], 0)
        far, at = (b3, j) if j < half else (b4, j - half)
        b = jnp.concatenate(
            [r[j * tg : (j + 1) * tg, :] for r in (b0, b1, b2)] + [far[at * tg : (at + 1) * tg, :]],
            0,
        )
        start = pl.multiple_of(row * BAND, 16)
        got_a = dot(pick_ref[row], a).astype(BF)
        got_b = dot(pick_ref[row], b).astype(BF)
        for e in range(2):
            out_ref[e, pl.ds(start, BAND), :width] = got_a[e * BAND : (e + 1) * BAND]
            out_ref[e, pl.ds(start, BAND), width:] = got_b[e * BAND : (e + 1) * BAND]


def pack_rows(pos, a_parts, b_parts, pick, blk, feats):
    tg = b_parts[0].shape[0] // SIDE
    specs = [pl.BlockSpec((p.shape[0], blk), lambda f, s: (0, f)) for p in a_parts + b_parts]
    return pl.pallas_call(
        functools.partial(pack_kernel, tg),
        out_shape=jax.ShapeDtypeStruct((2, ROWS, feats), BF),
        grid_spec=pltpu.PrefetchScalarGridSpec(
            num_scalar_prefetch=1,
            grid=(feats // (2 * blk),),
            in_specs=specs + [pl.BlockSpec(pick.shape, lambda f, s: (0, 0, 0))],
            out_specs=pl.BlockSpec((2, ROWS, 2 * blk), lambda f, s: (0, 0, f)),
        ),
        compiler_params=pltpu.CompilerParams(vmem_limit_bytes=56 * MIB),
        cost_estimate=pl.CostEstimate(
            flops=2 * 2 * ROWS * SIDE * tg * feats, transcendentals=0, bytes_accessed=14 * 2**20
        ),
        name="pack",
    )(pos, *a_parts, *b_parts, pick)


def pack_plain_kernel(rows_ref, pick_ref, out_ref):
    got = dot(pick_ref[0], rows_ref[...]).astype(BF)
    for e in range(2):
        out_ref[e] = got[e * BAND : (e + 1) * BAND]


def pack_plain(rows, pick, feats, blk=2048):
    depth = pick.shape[2]
    return pl.pallas_call(
        pack_plain_kernel,
        out_shape=jax.ShapeDtypeStruct((2, ROWS, feats), BF),
        grid=(SIDE, feats // blk),
        in_specs=[
            pl.BlockSpec((depth, blk), lambda y, f: (y, f)),
            pl.BlockSpec((1, 2 * BAND, depth), lambda y, f: (y, 0, 0)),
        ],
        out_specs=pl.BlockSpec((2, BAND, blk), lambda y, f: (0, y, f)),
        compiler_params=pltpu.CompilerParams(vmem_limit_bytes=56 * MIB),
        cost_estimate=pl.CostEstimate(flops=1, transcendentals=0, bytes_accessed=1),
        name="pack_plain",
    )(rows, pick)


def own_at(n):
    return lambda e, j, s: (e, 0, jnp.minimum(j, n - 1))


def other_at(n):
    return lambda e, j, s: (e, 0, jnp.maximum(j - n, 0))


def col_at(n):
    def at(e, j, s):
        first = j < n
        core = jnp.where(first, s[1], 1 - s[1])
        return (e, 0, core * n + jnp.where(first, j, j - n))

    return at


def pre_kernel(core_ref, own, other, wg, wu, out, x_buf, w_buf, sems):
    core = core_ref[0]
    hid = wg.shape[1]
    feats = own.shape[2]
    lo = pl.multiple_of(core * feats, feats)
    hi = pl.multiple_of((1 - core) * feats, feats)
    copies = []
    for e in range(2):
        copies += [
            pltpu.make_async_copy(own.at[e], x_buf.at[e, :, pl.ds(lo, feats)], sems.at[4 * e]),
            pltpu.make_async_copy(wg.at[e], w_buf.at[e, pl.ds(0, hid)], sems.at[4 * e + 1]),
            pltpu.make_async_copy(wu.at[e], w_buf.at[e, pl.ds(hid, hid)], sems.at[4 * e + 2]),
            pltpu.make_async_copy(other.at[e], x_buf.at[e, :, pl.ds(hi, feats)], sems.at[4 * e + 3]),
        ]
    for c in copies:
        c.start()
    for e in range(2):
        for c in copies[4 * e : 4 * e + 4]:
            c.wait()
        out[e] = dot_t(x_buf[e], w_buf[e])


ANY = pl.BlockSpec(memory_space=pl.ANY)
IN_VMEM = pl.BlockSpec(memory_space=pltpu.VMEM)
IN_SMEM = pl.BlockSpec(memory_space=pltpu.SMEM)


def pre_rows(core, own, other, w_gate, w_up):
    hid, width = w_gate.shape[1:]
    return pl.pallas_call(
        pre_kernel,
        out_shape=jax.ShapeDtypeStruct((2, ROWS, 2 * hid), F32),
        in_specs=[IN_SMEM, ANY, ANY, ANY, ANY],
        out_specs=IN_VMEM,
        scratch_shapes=[
            pltpu.VMEM((2, ROWS, width), BF),
            pltpu.VMEM((2, 2 * hid, width), BF),
            pltpu.SemaphoreType.DMA((8,)),
        ],
        compiler_params=pltpu.CompilerParams(vmem_limit_bytes=56 * MIB),
        cost_estimate=pl.CostEstimate(
            flops=2 * 4 * ROWS * hid * width, transcendentals=0, bytes_accessed=18 * 2**20
        ),
        name="pre",
    )(core, own, other, w_gate, w_up)


def mid_kernel(
    core_ref, own, other, wd, wg, wu, pre, g_ref,
    dx_a, keep_b, send_b, both_o, hid_o, score,
    y_buf, d_buf, w_buf, dx_buf, few_buf, sems, out_sems,
):
    core = core_ref[0]
    hid, width = wd.shape[1:]
    feats = own.shape[2]
    part = width // 8
    few = part // 4
    lo = pl.multiple_of(core * feats, feats)
    hi = pl.multiple_of((1 - core) * feats, feats)
    order = (1, 0)
    copies = {}
    for e in order:
        copies[e] = [
            pltpu.make_async_copy(wd.at[e], d_buf.at[e], sems.at[5 * e]),
            pltpu.make_async_copy(own.at[e], y_buf.at[e, :, pl.ds(lo, feats)], sems.at[5 * e + 1]),
            pltpu.make_async_copy(other.at[e], y_buf.at[e, :, pl.ds(hi, feats)], sems.at[5 * e + 2]),
            pltpu.make_async_copy(wg.at[e], w_buf.at[e, pl.ds(0, hid)], sems.at[5 * e + 3]),
            pltpu.make_async_copy(wu.at[e], w_buf.at[e, pl.ds(hid, hid)], sems.at[5 * e + 4]),
        ]
    for c in copies[order[0]][:3]:
        c.start()
    ends = []
    for e in order:
        gate, up, g = pre[e, :, :hid], pre[e, :, hid:], g_ref[e]
        s = jax.nn.sigmoid(gate)
        act = gate * s
        hidden = act * up
        slope = up * s * (1.0 + gate * (1.0 - s))
        hid_o[e] = (hidden * g).astype(BF)
        for c in copies[e][:3]:
            c.wait()
        if e == order[0]:
            for c in copies[order[0]][3:] + copies[order[1]]:
                c.start()
        dy = dot_t(y_buf[e], d_buf[e])
        score[e] = jnp.sum(hidden * dy, axis=1, keepdims=True)
        d_hid = dy * g
        both = jnp.concatenate([d_hid * slope, d_hid * act], 1)
        both_o[e] = both.astype(BF)
        for c in copies[e][3:]:
            c.wait()
        if e == 0:
            left = both.astype(BF)
            for k in range(8):
                cols = pl.ds(k * part, part)
                dx_buf[e, pl.ds(0, ROWS), cols] = dot(left, w_buf[e, :, cols]).astype(BF)
                c = pltpu.make_async_copy(
                    dx_buf.at[e, pl.ds(0, ROWS), cols],
                    dx_a.at[k, :, pl.ds(0, part)],
                    out_sems.at[8 + k],
                )
                c.start()
                ends.append(c)
        else:
            gap = jnp.zeros((PAD - CAP, 2 * hid), F32)
            rows = []
            for i in range(SIDE * SIDE):
                rows += [both[i * CAP : (i + 1) * CAP], gap]
            left = jnp.concatenate(rows, 0).astype(BF)
            for k in range(8):
                cols = pl.ds(k * part + few, part - few)
                to = pl.ds(k // 2 * (part - few), part - few)
                dx_buf[e, :, cols] = dot(left, w_buf[e, :, cols]).astype(BF)
                kept = pltpu.make_async_copy(dx_buf.at[e, :, cols], keep_b.at[:, to], out_sems.at[k])
                sent = pltpu.make_async_copy(dx_buf.at[e, :, cols], send_b.at[:, to], out_sems.at[k])

                @pl.when(core == k % 2)
                def _():
                    kept.start()

                @pl.when(core != k % 2)
                def _():
                    sent.start()

                ends.append(kept)
            left = both.astype(BF)
            for k in range(8):
                at = pl.ds(k * few, few)
                few_buf[:, at] = dot(left, w_buf[e, :, pl.ds(k * part, few)]).astype(BF)
                c = pltpu.make_async_copy(
                    few_buf.at[:, at],
                    dx_a.at[k, :, pl.ds(part, few)],
                    out_sems.at[16 + k],
                )
                c.start()
                ends.append(c)
    for c in ends:
        c.wait()


def mid_rows(core, own, other, w_down, w_gate, w_up, pre, g):
    hid, width = w_down.shape[1:]
    tall = SIDE * SIDE * PAD
    return pl.pallas_call(
        mid_kernel,
        out_shape=[
            jax.ShapeDtypeStruct((8, ROWS, width // 8 + width // 32), BF),
            jax.ShapeDtypeStruct((tall, width * 3 // 8), BF),
            jax.ShapeDtypeStruct((tall, width * 3 // 8), BF),
            jax.ShapeDtypeStruct((2, ROWS, 2 * hid), BF),
            jax.ShapeDtypeStruct((2, ROWS, hid), BF),
            jax.ShapeDtypeStruct((2, ROWS, 1), F32),
        ],
        in_specs=[IN_SMEM, ANY, ANY, ANY, ANY, ANY, IN_VMEM, IN_VMEM],
        out_specs=[ANY, ANY, ANY, IN_VMEM, IN_VMEM, IN_VMEM],
        scratch_shapes=[
            pltpu.VMEM((2, ROWS, width), BF),
            pltpu.VMEM((2, hid, width), BF),
            pltpu.VMEM((2, 2 * hid, width), BF),
            pltpu.VMEM((2, tall, width), BF),
            pltpu.VMEM((ROWS, width // 4), BF),
            pltpu.SemaphoreType.DMA((10,)),
            pltpu.SemaphoreType.DMA((24,)),
        ],
        compiler_params=pltpu.CompilerParams(vmem_limit_bytes=56 * MIB),
        cost_estimate=pl.CostEstimate(
            flops=2 * 6 * ROWS * hid * width,
            transcendentals=2 * ROWS * hid,
            bytes_accessed=34 * 2**20,
        ),
        name="mid",
    )(core, own, other, w_down, w_gate, w_up, pre, g)


def grad_kernel(n, pos_ref, x_own, x_other, y_own, y_other, both_o, hid_o, gg, gu, gd):
    j = pl.program_id(1)
    hid = gg.shape[1]

    def put(x, y):
        r = t_dot(both_o[0], x)
        gg[0] = r[:hid].astype(BF)
        gu[0] = r[hid:].astype(BF)
        gd[0] = t_dot(hid_o[0], y).astype(BF)

    @pl.when(j < n)
    def _():
        put(x_own[0], y_own[0])

    @pl.when(j >= n)
    def _():
        put(x_other[0], y_other[0])


def grad_rows(pos, x_own, x_other, y_own, y_other, both_o, hid_o, blk=1024):
    hid = hid_o.shape[2]
    n = x_own.shape[2] // blk
    whole = lambda e, j, s: (e, 0, 0)
    return pl.pallas_call(
        functools.partial(grad_kernel, n),
        out_shape=[jax.ShapeDtypeStruct((2, hid, 2 * n * blk), BF)] * 3,
        grid_spec=pltpu.PrefetchScalarGridSpec(
            num_scalar_prefetch=1,
            grid=(2, 2 * n),
            in_specs=[
                pl.BlockSpec((1, ROWS, blk), own_at(n)),
                pl.BlockSpec((1, ROWS, blk), other_at(n)),
                pl.BlockSpec((1, ROWS, blk), own_at(n)),
                pl.BlockSpec((1, ROWS, blk), other_at(n)),
                pl.BlockSpec((1, ROWS, 2 * hid), whole),
                pl.BlockSpec((1, ROWS, hid), whole),
            ],
            out_specs=[pl.BlockSpec((1, hid, blk), col_at(n))] * 3,
        ),
        compiler_params=pltpu.CompilerParams(vmem_limit_bytes=56 * MIB),
        cost_estimate=pl.CostEstimate(
            flops=2 * 6 * ROWS * hid * n * 2 * blk, transcendentals=0, bytes_accessed=30 * 2**20
        ),
        name="grads",
    )(pos, x_own, x_other, y_own, y_other, both_o, hid_o)


def before_count(member):
    t = member.shape[-1]
    upper = (jnp.arange(t)[:, None] < jnp.arange(t)[None, :]).astype(BF)
    return jnp.dot(member.astype(BF), upper, preferred_element_type=F32).astype(jnp.int32)


def on_device(tokens, cotangent, gate_values, expert_ids, w_gate, w_up, w_down):
    tg, top = expert_ids.shape
    width = tokens.shape[1]
    n_exp = lax.axis_size("expert")
    experts = 2 * n_exp
    me = lax.axis_index("expert")
    lane = lax.axis_index("tensor")
    y, z, core = me // SIDE, me % SIDE, lane % 2
    pos = jnp.stack([y, core]).astype(jnp.int32)
    feats = width // 2
    blk = 512

    def half(v):
        return lax.dynamic_slice_in_dim(v, core * feats, feats, 1)

    x_all = lax.all_gather(half(tokens), "expert", axis=0, tiled=True)
    y_half = half(cotangent).reshape(tg, feats // (2 * blk), 2, blk)
    ya = y_half[:, :, 0].reshape(tg, feats // 2)
    yb = y_half[:, :, 1].reshape(tg, feats // 2)
    ya1 = jnp.concatenate(ring(ya, "z"), 0)
    yb1 = jnp.concatenate(ring(yb, "y"), 0)
    ya_parts, yb_parts = near(ya1, "y"), near(yb1, "z")

    route = jnp.concatenate([expert_ids.astype(BF), gate_values], 1)
    route = route.reshape(2 * tg * top // 128, 128)
    route = after_all(jnp.tile(route, (n_exp, 1)), (ya_parts, yb_parts))
    route = lax.all_to_all(route, "expert", split_axis=0, concat_axis=0, tiled=True)
    tab = route.reshape(SIDE, SIDE, tg, 2 * top)
    ids = tab[..., :top].astype(jnp.int32)
    gates = tab[..., top:].astype(F32)
    mine = 2 * me + jnp.arange(2)
    named = ids[None] == mine[:, None, None, None, None]
    member = jnp.any(named, -1)
    weight = jnp.sum(jnp.where(named, gates[None], 0.0), -1)
    count = before_count(member)
    target = jnp.where(member, jnp.arange(SIDE)[None, None, :, None] * CAP + count, -1)

    def hits(v):
        return v.reshape(2, SIDE, 1, SIDE * tg) == jnp.arange(BAND)[None, None, :, None]

    def picks(v):
        return hits(v).astype(BF).transpose(1, 0, 2, 3).reshape(SIDE, 2 * BAND, SIDE * tg)

    pick = picks(target)
    pick_ring = picks(target[:, :, (z + jnp.array(OFFS)) % SIDE])
    g_slot = jnp.sum(jnp.where(hits(target), weight.reshape(2, SIDE, 1, SIDE * tg), 0.0), -1)
    g_slot = g_slot.reshape(2, ROWS, 1)

    ya_parts, yb_parts = ya_parts + far(ya_parts, "y"), yb_parts + far(yb_parts, "z")
    x_own = pack_plain(x_all, pick, feats)
    x_other = swap_core(x_own)
    ya_parts, yb_parts = after_all((ya_parts, yb_parts), x_own)
    y_own = pack_rows(pos, ya_parts, yb_parts, pick_ring, blk, feats)
    pre = pre_rows(core.astype(jnp.int32).reshape(1), x_own, x_other, w_gate, w_up)
    cores = core.astype(jnp.int32).reshape(1)
    y_other = swap_core(y_own)
    dx_a, keep_b, send_b, both_o, hid_o, score = mid_rows(
        cores, y_own, y_other, w_down, w_gate, w_up, pre, g_slot
    )

    n_ten = lax.axis_size("tensor")
    part = width // n_ten
    few = part // 4
    rest = part - few
    share = lax.psum_scatter(dx_a, "tensor", scatter_dimension=0, tiled=True)
    came = swap_core(send_b)
    out_b = (keep_b.astype(F32) + came.astype(F32)).astype(BF)
    back_b = lax.all_to_all(out_b, "expert", split_axis=0, concat_axis=0, tiled=True)
    both_o, hid_o = after_all((both_o, hid_o), out_b)
    grads = grad_rows(pos, x_own, x_other, y_own, y_other, both_o, hid_o)

    total = score.reshape(ROWS * 2 // 128, 128)
    for bit in (1, 2, 4):
        total = total + lax.ppermute(total, "tensor", [(i, i ^ bit) for i in range(n_ten)])

    own_named = expert_ids[:, :, None] == jnp.arange(experts)[None, None, :]
    own_member = jnp.any(own_named, 1)
    own_count = before_count(own_member.T).T
    own_hit = own_member[:, :, None] & (own_count[:, :, None] == jnp.arange(PAD)[None, None, :])
    spread = own_hit.astype(BF).reshape(tg, n_exp, 2, PAD)
    spread_a, spread_b = spread[:, :, 0], spread[:, :, 1]

    line = total.reshape(2, n_exp, CAP).transpose(1, 0, 2).reshape(n_exp, 1, 2 * CAP).astype(BF)
    line = jnp.pad(line, ((0, 0), (0, PAD - CAP - 1), (0, part + few - 2 * CAP)))
    back = jnp.concatenate([share.reshape(n_exp, CAP, part + few), line], 1)
    back, grads = lax.optimization_barrier((back, grads))
    back = lax.all_to_all(back, "expert", split_axis=0, concat_axis=0, tiled=True)
    sum_b = jnp.einsum(
        "tns,nsf->tf",
        spread_b,
        back_b.reshape(n_exp, PAD, width * 3 // 8),
        preferred_element_type=F32,
    ).astype(BF)
    x = lane // 2
    mine_b = lax.dynamic_slice_in_dim(sum_b, x * rest, rest, 1).astype(F32)
    for step in range(1, n_ten // 2):
        piece = lax.dynamic_slice_in_dim(sum_b, (x + step) % (n_ten // 2) * rest, rest, 1)
        perm = [(i, (i + 2 * step) % n_ten) for i in range(n_ten)]
        mine_b = mine_b + lax.ppermute(piece, "tensor", perm).astype(F32)

    sum_a = jnp.einsum("tns,nsf->tf", spread_a, back[:, :, :part], preferred_element_type=F32)
    sum_few = jnp.einsum("tns,nsf->tf", spread_b, back[:, :, part:], preferred_element_type=F32)
    d_tokens = (sum_a + jnp.concatenate([sum_few, mine_b], 1)).astype(BF)
    scores = back[:, CAP, : 2 * CAP].reshape(experts, CAP).astype(F32)
    by_expert = jnp.sum(jnp.where(own_hit[:, :, :CAP], scores[None], 0.0), 2)
    d_gates = jnp.sum(jnp.where(own_named, by_expert[:, None, :], 0.0), 2).astype(BF)
    return (d_tokens, d_gates) + tuple(grads)


def solution(mesh):
    placed = (
        P("expert", None),
        P("expert", None),
        P("expert", None),
        P("expert", None),
        P("expert", "tensor", None),
        P("expert", "tensor", None),
        P("expert", "tensor", None),
    )
    return jax.shard_map(
        on_device,
        mesh=mesh,
        in_specs=placed,
        out_specs=(
            P("expert", "tensor"),
            P("expert", None),
            P("expert", "tensor", None),
            P("expert", "tensor", None),
            P("expert", "tensor", None),
        ),
        check_vma=False,
    )
```
